512 devices in a mesh: dp: 32 (over y, x, core), tensor: 16 (over z).
Axes of the slice: x: 4, y: 4, z: 16, core: 2. Of those that a mesh axis runs over, the one named last changes fastest.
Arguments:
- gradient: bfloat16 [32, 384, 28672], P('dp', None, 'tensor'), may hold values from -80 to 80
- error: bfloat16 [32, 384, 28672], P('dp', None, 'tensor'), may hold values from -3 to 3
- q_prev: bfloat16 [28672, 128], P('tensor'), may hold values from -6 to 6
Outputs:
- new_error: bfloat16 [32, 384, 28672], P('dp', None, 'tensor')
- q_next: bfloat16 [28672, 128], P('tensor')
The draws below stay inside these ranges and needn't reach their ends.
All inputs are finite; a program needn't handle non-finite values.
Results may differ from the reference program's by a relative error of at most 0.013.
Values may be sent and summed in bfloat16 or wider, within the bound.
No kernel may reach another device: no remote copies, remote signals or barrier semaphores. Data moves between devices by JAX's collectives and lax.ppermute only.
A program may use at most 64 MiB of HBM per device.

```python
import jax
import jax.numpy as jnp
from jax import lax

COLS = 28672
ROWS = 384
RANK = 128
N_DP = 32


def draw_gradient(key, part):
    key = jax.random.fold_in(key, 11)
    keys = jax.random.split(key, 4)
    row_scale = jnp.exp(jax.random.uniform(keys[0], (1, ROWS, 1), jnp.float32, jnp.log(0.3), jnp.log(3.0)))
    col_scale = jnp.exp(jax.random.uniform(keys[1], (1, 1, COLS), jnp.float32, jnp.log(0.3), jnp.log(3.0)))
    common = jax.random.normal(keys[2], (1, ROWS, COLS), jnp.float32)
    noise = jax.random.normal(keys[3], (N_DP, ROWS, COLS), jnp.float32)
    values = row_scale * col_scale * (common + noise)
    return jnp.clip(values, -80.0, 80.0).astype(jnp.bfloat16)


def block_scale(own_key, dims, cuts, smallest, largest):
    level, own = 1.0, jax.random.fold_in(own_key, 6)
    for axis_at, blocks in cuts:
        draws = jnp.exp(jax.random.uniform(jax.random.fold_in(own, axis_at), (blocks,), jnp.float32, smallest / len(cuts), largest / len(cuts)))
        level = level * jnp.repeat(draws, dims[axis_at] // blocks).reshape([-1 if axis == axis_at else 1 for axis in range(len(dims))])
    return level


def scatter_about(stream_key, extent, scale, bound, cuts=(), kind=jnp.bfloat16):
    factor_of = block_scale(stream_key, extent, cuts, -0.22, 0.18) if cuts else 1.0
    values = jax.random.normal(stream_key, extent, jnp.float32) * scale * factor_of
    return jnp.minimum(jnp.maximum(values, -bound), bound).astype(kind)


def setup_inputs(seed: int = 0) -> dict:
    arg_keys = jax.random.split(jax.random.key(seed), 4)
    return {
        "gradient": draw_gradient(jax.random.fold_in(arg_keys[3], 71), 0),
        "error": scatter_about(arg_keys[1], (N_DP, ROWS, COLS), 0.5, 3.0, ((0, 32), (2, 16))),
        "q_prev": scatter_about(arg_keys[2], (COLS, RANK), 1.0, 6.0, ((0, 16),)),
    }


def reference(gradient, error, q_prev):
    combined = (gradient.astype(jnp.float32) + error.astype(jnp.float32)).astype(jnp.bfloat16)
    p_terms = lax.map(lambda block: jnp.dot(block.astype(jnp.float32), q_prev.astype(jnp.float32), preferred_element_type=jnp.float32), combined)
    p_sum = jnp.sum(p_terms, axis=0)
    gram = jnp.dot(p_sum.T, p_sum, precision=lax.Precision.HIGHEST)
    lower = jnp.linalg.cholesky(gram)
    basis = lax.linalg.triangular_solve(lower, p_sum, left_side=False, lower=True, transpose_a=True).astype(jnp.bfloat16)

    def right_term(block):
        return lax.dot_general(block.astype(jnp.float32), basis.astype(jnp.float32), (((0,), (0,)), ((), ())), preferred_element_type=jnp.float32)
    q_terms = lax.map(right_term, combined)
    q_next = (jnp.sum(q_terms, axis=0) / N_DP).astype(jnp.bfloat16)
    decompressed = lax.dot_general(basis.astype(jnp.float32), q_next.astype(jnp.float32), (((1,), (1,)), ((), ())), preferred_element_type=jnp.float32)
    new_error = (combined.astype(jnp.float32) - decompressed[None]).astype(jnp.bfloat16)
    return (new_error, q_next)
```

```python
import jax
import jax.numpy as jnp
from jax import lax
from jax.sharding import PartitionSpec as P


def exchange(pieces, axis):
    return lax.all_to_all(pieces, axis, 0, 0)


def gather(piece, axis):
    return exchange(jnp.broadcast_to(piece[None], (lax.axis_size(axis),) + piece.shape), axis)


def orthonormal(p_block, gram):
    lower = jnp.linalg.cholesky(gram)
    return lax.linalg.triangular_solve(
        lower, p_block, left_side=False, lower=True, transpose_a=True
    ).astype(jnp.bfloat16)


def on_device(gradient, error, q_prev):
    rows, cols = gradient.shape[1:]
    rank = q_prev.shape[1]
    replicas = lax.axis_size("dp")
    slabs = cols // rank
    combined = (gradient[0].astype(jnp.float32) + error[0].astype(jnp.float32)).astype(jnp.bfloat16)
    p_local = jnp.dot(combined, q_prev, preferred_element_type=jnp.float32)
    slabbed = combined.reshape(rows, slabs, rank).transpose(1, 0, 2).reshape(replicas, -1, rank)

    p_pieces = exchange(jnp.pad(p_local, ((0, 128), (0, 0))).reshape(replicas, -1, rank), "dp")
    p_piece = jnp.sum(gather(jnp.sum(p_pieces, axis=0), "tensor"), axis=0)
    p_sum = gather(p_piece, "dp").reshape(-1, rank)[:rows]

    total_piece = jnp.sum(exchange(slabbed, "dp").astype(jnp.float32), axis=0).astype(jnp.bfloat16)
    total = gather(total_piece, "dp").reshape(slabs, rows, rank)

    gram = jnp.dot(p_sum.T, p_sum, precision=lax.Precision.HIGHEST)
    basis = orthonormal(p_sum, gram)
    q_total = jnp.einsum("src,rk->sck", total, basis, preferred_element_type=jnp.float32).reshape(cols, rank)
    q_next = (q_total / replicas).astype(jnp.bfloat16)
    decompressed = lax.dot_general(
        basis, q_next, (((1,), (1,)), ((), ())), preferred_element_type=jnp.float32
    )
    new_error = (combined.astype(jnp.float32) - decompressed).astype(jnp.bfloat16)
    return (new_error[None], q_next)


def solution(mesh):
    placed = (P("dp", None, "tensor"), P("dp", None, "tensor"), P("tensor", None))
    return jax.shard_map(
        on_device,
        mesh=mesh,
        in_specs=placed,
        out_specs=(P("dp", None, "tensor"), P("tensor", None)),
        check_vma=False,
    )
```

```python
import jax
import jax.numpy as jnp
from jax import lax
from jax.experimental import pallas as pl
from jax.experimental.pallas import tpu as pltpu
from jax.sharding import PartitionSpec as P

F32, BF16 = jnp.float32, jnp.bfloat16
LANES = 128
CHIPS = 16
STEP = 16
VMEM_LIMIT = 48 * 1024 * 1024


def params():
    return pltpu.CompilerParams(vmem_limit_bytes=VMEM_LIMIT)


def split(x):
    high = x.astype(BF16)
    return high, (x - high.astype(F32)).astype(BF16)


def whole(shape):
    return pl.BlockSpec(shape, lambda *_: (0,) * len(shape))


def combine_kernel(core_ref, g_ref, e_ref, own_ref, other_ref):
    core = core_ref[0]
    half = g_ref.shape[0] // 2
    for slab in range(g_ref.shape[1] // LANES):
        columns = slice(slab * LANES, (slab + 1) * LANES)
        for which, out_ref in ((core, own_ref), (1 - core, other_ref)):
            rows = pl.ds(pl.multiple_of(which * half, half), half)
            total = g_ref[rows, columns].astype(F32) + e_ref[rows, columns].astype(F32)
            out_ref[slab * half : (slab + 1) * half, :] = total.astype(BF16)


def combine(core, gradient, error):
    rows, cols = gradient.shape
    steps = 2
    slabs = cols // LANES
    out = jax.ShapeDtypeStruct((slabs * rows // 2, LANES), BF16)
    block = pl.BlockSpec((rows, cols // steps), lambda i: (0, i))
    out_block = pl.BlockSpec((slabs // steps * rows // 2, LANES), lambda i: (i, 0))
    return pl.pallas_call(
        combine_kernel,
        grid=(steps,),
        out_shape=(out, out),
        in_specs=[pl.BlockSpec(memory_space=pltpu.SMEM), block, block],
        out_specs=(out_block, out_block),
        compiler_params=params(),
        name="combine",
    )(core, gradient, error)


def pack_kernel(own_ref, got_ref, q_ref, out_ref):
    half = own_ref.shape[0] // (q_ref.shape[0] // LANES)
    span = out_ref.shape[1] - 2 * STEP
    p = jnp.zeros((half, LANES), F32)
    for slab in range(q_ref.shape[0] // LANES):
        rows = slice(slab * half, (slab + 1) * half)
        q = q_ref[slab * LANES : (slab + 1) * LANES, :]
        both = jnp.concatenate([own_ref[rows, :], got_ref[rows, :]], axis=1)
        p += jnp.dot(both, jnp.concatenate([q, q], axis=0), preferred_element_type=F32)
    high, low = split(p)
    for piece in range(CHIPS):
        if (piece + 1) * STEP <= half:
            out_ref[piece, :STEP, :] = high[piece * STEP : (piece + 1) * STEP, :]
            out_ref[piece, STEP : 2 * STEP, :] = low[piece * STEP : (piece + 1) * STEP, :]
        else:
            out_ref[piece, : 2 * STEP, :] = jnp.zeros((2 * STEP, LANES), BF16)
        first = piece * span
        count = min(span, own_ref.shape[0] - first)
        total = own_ref[first : first + count, :].astype(F32) + got_ref[first : first + count, :].astype(F32)
        out_ref[piece, 2 * STEP : 2 * STEP + count, :] = total.astype(BF16)
        if count < span:
            out_ref[piece, 2 * STEP + count :, :] = jnp.zeros((span - count, LANES), BF16)


def pack(own, got, q_prev, span):
    return pl.pallas_call(
        pack_kernel,
        out_shape=jax.ShapeDtypeStruct((CHIPS, 2 * STEP + span, LANES), BF16),
        compiler_params=params(),
        name="pack",
    )(own, got, q_prev)


def left_piece_kernel(in_ref, out_ref):
    total = in_ref[0, :STEP, :].astype(F32) + in_ref[0, STEP:, :].astype(F32)
    for chip in range(1, CHIPS):
        total += in_ref[chip, :STEP, :].astype(F32) + in_ref[chip, STEP:, :].astype(F32)
    for copy in range(out_ref.shape[0]):
        out_ref[copy] = total


def left_piece(pieces, copies):
    return pl.pallas_call(
        left_piece_kernel,
        grid=(1,),
        out_shape=jax.ShapeDtypeStruct((copies, STEP, LANES), F32),
        in_specs=[whole((CHIPS, 2 * STEP, LANES))],
        out_specs=whole((copies, STEP, LANES)),
        compiler_params=params(),
        name="left_piece",
    )(pieces)


def total_piece_kernel(in_ref, out_ref):
    total = in_ref[0, 2 * STEP :, :].astype(F32)
    for chip in range(1, CHIPS):
        total += in_ref[chip, 2 * STEP :, :].astype(F32)
    out_ref[...] = total.astype(BF16)


def total_piece(pieces):
    return pl.pallas_call(
        total_piece_kernel,
        out_shape=jax.ShapeDtypeStruct((pieces.shape[1] - 2 * STEP, LANES), BF16),
        compiler_params=params(),
        name="total_piece",
    )(pieces)


def repack_kernel(left_ref, total_ref, out_ref):
    p = left_ref[0]
    for at in range(1, left_ref.shape[0]):
        p += left_ref[at]
    high, low = split(p)
    total = total_ref[...]
    for chip in range(CHIPS):
        out_ref[chip, :STEP, :] = high
        out_ref[chip, STEP : 2 * STEP, :] = low
        out_ref[chip, 2 * STEP :, :] = total


def repack(left, total):
    return pl.pallas_call(
        repack_kernel,
        out_shape=jax.ShapeDtypeStruct((CHIPS, 2 * STEP + total.shape[0], LANES), BF16),
        compiler_params=params(),
        name="repack",
    )(left, total)


def left_half_kernel(in_ref, out_ref):
    for piece in range(out_ref.shape[0] // STEP):
        out_ref[piece * STEP : (piece + 1) * STEP, :] = in_ref[piece, :STEP, :].astype(F32) + in_ref[
            piece, STEP:, :
        ].astype(F32)


def left_half(pieces, half):
    return pl.pallas_call(
        left_half_kernel,
        grid=(1,),
        out_shape=jax.ShapeDtypeStruct((half, LANES), F32),
        in_specs=[whole((CHIPS, 2 * STEP, LANES))],
        out_specs=whole((half, LANES)),
        compiler_params=params(),
        name="left_half",
    )(pieces)


def spread(x, row=None, lane=None):
    if row is not None:
        x = x[row : row + 1, :]
    if lane is not None:
        x = x[:, lane : lane + 1]
    return jnp.broadcast_to(x, (8, LANES))


def inverse_factor(gram):
    groups = LANES // 8
    a = [gram[8 * g : 8 * g + 8, :] for g in range(groups)]
    row_of = lax.broadcasted_iota(jnp.int32, (8, LANES), 0)
    lane_of = lax.broadcasted_iota(jnp.int32, (8, LANES), 1)
    inv = [jnp.where(lane_of == row_of + 8 * g, 1.0, 0.0).astype(F32) for g in range(groups)]
    width = 4
    for first in range(0, LANES, width):
        g, s = first // 8, first % 8
        column = {h: [spread(a[h], lane=first + i) for i in range(width)] for h in range(g, groups)}
        d = [[spread(column[g][i], row=s + m) for i in range(m + 1)] for m in range(width)]
        low = [[None] * width for _ in range(width)]
        root = [None] * width
        for i in range(width):
            pivot = d[i][i]
            for k in range(i):
                pivot = pivot - low[i][k] * low[i][k]
            root[i] = lax.rsqrt(pivot)
            for m in range(i + 1, width):
                value = d[m][i]
                for k in range(i):
                    value = value - low[m][k] * low[i][k]
                low[m][i] = value * root[i]

        def solve(rows):
            y = []
            for m in range(width):
                value = rows[m]
                for k in range(m):
                    value = value - low[m][k] * y[k]
                y.append(value * root[m])
            z = [None] * width
            for m in reversed(range(width)):
                value = y[m]
                for k in range(m + 1, width):
                    value = value - low[k][m] * z[k]
                z[m] = value * root[m]
            return y, z

        _, za = solve([spread(a[g], row=s + m) for m in range(width)])
        yi, zi = solve([spread(inv[g], row=s + m) for m in range(width)])
        for h in range(g, groups):
            if h > g or s + width < 8:
                new_a, new_inv = a[h], inv[h]
                for i in range(width):
                    new_a = new_a - column[h][i] * za[i]
                    new_inv = new_inv - column[h][i] * zi[i]
                a[h] = new_a
                if h > g:
                    inv[h] = new_inv
                else:
                    inv[h] = jnp.where(row_of >= s + width, new_inv, inv[h])
        for m in range(width):
            inv[g] = jnp.where(row_of == s + m, yi[m], inv[g])
    return jnp.concatenate(inv, axis=0)


def basis_kernel(own_ref, other_ref, out_ref):
    def gram_of(p):
        return lax.dot_general(
            p, p, (((0,), (0,)), ((), ())), precision=lax.Precision.HIGHEST, preferred_element_type=F32
        )

    own, other = own_ref[...], other_ref[...]
    inverse = inverse_factor(gram_of(own) + gram_of(other))
    for at, p in enumerate((own, other)):
        out_ref[at] = lax.dot_general(
            p, inverse, (((1,), (1,)), ((), ())), precision=lax.Precision.HIGHEST, preferred_element_type=F32
        ).astype(BF16)


def bases(own, other):
    return pl.pallas_call(
        basis_kernel,
        out_shape=jax.ShapeDtypeStruct((2,) + own.shape, BF16),
        compiler_params=params(),
        cost_estimate=pl.CostEstimate(flops=20_000_000, bytes_accessed=15_000_000, transcendentals=0),
        name="basis",
    )(own, other)


def finish_kernel(replicas, core_ref, own_ref, other_ref, own_sum_ref, other_sum_ref, basis_ref, error_ref, q_ref):
    core = core_ref[0]
    half = basis_ref.shape[1]
    span = own_sum_ref.shape[1] - 2 * STEP

    def slab_of(ref, slab):
        at, end, parts = slab * half, (slab + 1) * half, []
        while at < end:
            piece = at // span
            stop = min(end, (piece + 1) * span)
            parts.append(ref[piece, 2 * STEP + at - piece * span : 2 * STEP + stop - piece * span, :])
            at = stop
        return jnp.concatenate(parts, axis=0)

    def pair_of(read, pair):
        return jnp.concatenate([read(2 * pair), read(2 * pair + 1)], axis=1)

    basis = (basis_ref[0], basis_ref[1])
    flipped = [b.astype(F32).T.astype(BF16) for b in basis]
    for pair in range(q_ref.shape[0] // (2 * LANES)):
        columns = slice(2 * pair * LANES, 2 * (pair + 1) * LANES)
        terms = [
            jnp.dot(flat, pair_of(lambda slab: slab_of(ref, slab), pair), preferred_element_type=F32)
            for flat, ref in zip(flipped, (own_sum_ref, other_sum_ref))
        ]
        scaled = (terms[0] + terms[1]) * (1.0 / replicas)
        q_ref[columns, :] = scaled.T.astype(BF16)
        right = scaled.astype(BF16)
        for which, ref, b in ((core, own_ref, basis[0]), (1 - core, other_ref, basis[1])):
            mine = pair_of(lambda slab: ref[slab * half : (slab + 1) * half, :], pair).astype(F32)
            rows = pl.ds(pl.multiple_of(which * half, half), half)
            error_ref[rows, columns] = (mine - jnp.dot(b, right, preferred_element_type=F32)).astype(BF16)


def finish(core, own, other, own_sum, other_sum, basis, replicas):
    rows, cols = 2 * basis.shape[1], own.shape[0] // basis.shape[1] * LANES
    vmem = pl.BlockSpec(memory_space=pltpu.VMEM)
    return pl.pallas_call(
        lambda *refs: finish_kernel(replicas, *refs),
        out_shape=(jax.ShapeDtypeStruct((rows, cols), BF16), jax.ShapeDtypeStruct((cols, LANES), BF16)),
        in_specs=[pl.BlockSpec(memory_space=pltpu.SMEM)] + [vmem] * 5,
        out_specs=(vmem, vmem),
        compiler_params=params(),
        name="finish",
    )(core, own, other, own_sum, other_sum, basis)


def on_device(gradient, error, q_prev):
    rows, cols = gradient.shape[1:]
    replicas = lax.axis_size("dp")
    half = rows // 2
    slab_rows = cols // LANES * half
    span = -(-slab_rows // CHIPS // 16) * 16
    core = (lax.axis_index("dp") % 2).astype(jnp.int32).reshape(1)
    twin = [(i, i ^ 1) for i in range(replicas)]
    same_core = [[2 * chip + c for chip in range(CHIPS)] for c in range(2)]

    def across_chips(pieces):
        return lax.all_to_all(pieces, "dp", 0, 0, axis_index_groups=same_core)

    own, other = combine(core, gradient[0], error[0])
    got = lax.ppermute(other, "dp", twin)
    pieces = across_chips(pack(own, got, q_prev, span))
    left = lax.all_to_all(left_piece(pieces, lax.axis_size("tensor")), "tensor", 0, 0)
    gathered = across_chips(repack(left, total_piece(pieces)))
    left_own = left_half(gathered, half)
    left_other = lax.ppermute(left_own, "dp", twin)
    gathered_other = lax.ppermute(gathered, "dp", twin)
    basis = bases(left_own, left_other)
    new_error, q_next = finish(core, own, other, gathered, gathered_other, basis, replicas)
    return (new_error[None], q_next)


def solution(mesh):
    placed = (P("dp", None, "tensor"), P("dp", None, "tensor"), P("tensor", None))
    return jax.shard_map(
        on_device,
        mesh=mesh,
        in_specs=placed,
        out_specs=(P("dp", None, "tensor"), P("tensor", None)),
        check_vma=False,
    )
```

```python
import jax
import jax.numpy as jnp
from jax import lax
from jax.experimental import pallas as pl
from jax.experimental.pallas import tpu as pltpu
from jax.sharding import PartitionSpec as P

F32, BF16 = jnp.float32, jnp.bfloat16
LANES = 128
CHIPS = 16
STEP = 16
VMEM_LIMIT = 48 * 1024 * 1024
SENT_LIMIT = 52 * 1024 * 1024
KEPT_LIMIT = 52 * 1024 * 1024


def params():
    return pltpu.CompilerParams(vmem_limit_bytes=VMEM_LIMIT)


def split(x):
    high = x.astype(BF16)
    return high, (x - high.astype(F32)).astype(BF16)


def combined_half(which, g_in, e_in, out_ref, g_ref, e_ref, sems):
    half, cols = g_ref.shape
    chunks = sems.shape[1]
    count = half // chunks
    copies = []
    for chunk in range(chunks):
        rows = pl.ds(pl.multiple_of(which * half + chunk * count, 16), count)
        here = slice(chunk * count, (chunk + 1) * count)
        pair = [
            pltpu.make_async_copy(g_in.at[rows, :], g_ref.at[here, :], sems.at[0, chunk]),
            pltpu.make_async_copy(e_in.at[rows, :], e_ref.at[here, :], sems.at[1, chunk]),
        ]
        for copy in pair:
            copy.start()
        copies.append(pair)
    for chunk in range(chunks):
        for copy in copies[chunk]:
            copy.wait()
        here = slice(chunk * count, (chunk + 1) * count)
        total = (g_ref[here, :].astype(F32) + e_ref[here, :].astype(F32)).astype(BF16)
        for slab in range(cols // LANES):
            first = slab * half + chunk * count
            out_ref[first : first + count, :] = total[:, slab * LANES : (slab + 1) * LANES]


def sent_kernel(core_ref, g_in, e_in, out_ref, *scratch):
    combined_half(1 - core_ref[0], g_in, e_in, out_ref, *scratch)


def kept_kernel(core_ref, g_in, e_in, q_ref, out_ref, p_ref, *scratch):
    combined_half(core_ref[0], g_in, e_in, out_ref, *scratch)
    p_ref[...] = slab_product(out_ref, q_ref, p_ref.shape[0])


def slab_product(slabs_ref, q_ref, half):
    p = jnp.zeros((half, LANES), F32)
    for pair in range(q_ref.shape[0] // (2 * LANES)):
        two = [slabs_ref[(2 * pair + k) * half : (2 * pair + k + 1) * half, :] for k in range(2)]
        q = q_ref[2 * pair * LANES : 2 * (pair + 1) * LANES, :]
        p += jnp.dot(jnp.concatenate(two, axis=1), q, preferred_element_type=F32)
    return p


def half_call(kernel, limit, core, gradient, error, *more):
    rows, cols = gradient.shape
    half = rows // 2
    chunks = 4
    out = jax.ShapeDtypeStruct((cols // LANES * half, LANES), BF16)
    vmem = pl.BlockSpec(memory_space=pltpu.VMEM)
    anywhere = pl.BlockSpec(memory_space=pl.ANY)
    return pl.pallas_call(
        kernel,
        out_shape=(out, jax.ShapeDtypeStruct((half, LANES), F32)) if more else out,
        in_specs=[pl.BlockSpec(memory_space=pltpu.SMEM), anywhere, anywhere] + [vmem] * len(more),
        out_specs=(vmem, vmem) if more else vmem,
        scratch_shapes=[
            pltpu.VMEM((half, cols), BF16),
            pltpu.VMEM((half, cols), BF16),
            pltpu.SemaphoreType.DMA((2, chunks)),
        ],
        compiler_params=pltpu.CompilerParams(vmem_limit_bytes=limit),
        name="kept" if more else "sent",
    )(core, gradient, error, *more)


def pack_kernel(own_ref, got_ref, p_ref, q_ref, out_ref):
    half = p_ref.shape[0]
    span = out_ref.shape[1] - 2 * STEP
    high, low = split(p_ref[...] + slab_product(got_ref, q_ref, half))
    for piece in range(CHIPS):
        if (piece + 1) * STEP <= half:
            out_ref[piece, :STEP, :] = high[piece * STEP : (piece + 1) * STEP, :]
            out_ref[piece, STEP : 2 * STEP, :] = low[piece * STEP : (piece + 1) * STEP, :]
        else:
            out_ref[piece, : 2 * STEP, :] = jnp.zeros((2 * STEP, LANES), BF16)
        first = piece * span
        count = min(span, own_ref.shape[0] - first)
        total = own_ref[first : first + count, :].astype(F32) + got_ref[first : first + count, :].astype(F32)
        out_ref[piece, 2 * STEP : 2 * STEP + count, :] = total.astype(BF16)
        if count < span:
            out_ref[piece, 2 * STEP + count :, :] = jnp.zeros((span - count, LANES), BF16)


def pack(own, got, p_own, q_prev, span):
    return pl.pallas_call(
        pack_kernel,
        out_shape=jax.ShapeDtypeStruct((CHIPS, 2 * STEP + span, LANES), BF16),
        compiler_params=params(),
        name="pack",
    )(own, got, p_own, q_prev)


def sums_kernel(in_ref, left_ref, total_ref):
    left = jnp.zeros(left_ref.shape[1:], F32)
    total = jnp.zeros(total_ref.shape, F32)
    for chip in range(CHIPS):
        left += in_ref[chip, :STEP, :].astype(F32) + in_ref[chip, STEP : 2 * STEP, :].astype(F32)
        total += in_ref[chip, 2 * STEP :, :].astype(F32)
    for copy in range(left_ref.shape[0]):
        left_ref[copy] = left
    total_ref[...] = total.astype(BF16)


def sums(pieces, copies):
    return pl.pallas_call(
        sums_kernel,
        out_shape=(
            jax.ShapeDtypeStruct((copies, STEP, LANES), F32),
            jax.ShapeDtypeStruct((pieces.shape[1] - 2 * STEP, LANES), BF16),
        ),
        compiler_params=params(),
        name="sums",
    )(pieces)


def repack_kernel(left_ref, total_ref, out_ref):
    p = left_ref[0]
    for at in range(1, left_ref.shape[0]):
        p += left_ref[at]
    high, low = split(p)
    total = total_ref[...]
    for chip in range(CHIPS):
        out_ref[chip, :STEP, :] = high
        out_ref[chip, STEP : 2 * STEP, :] = low
        out_ref[chip, 2 * STEP :, :] = total


def repack(left, total):
    return pl.pallas_call(
        repack_kernel,
        out_shape=jax.ShapeDtypeStruct((CHIPS, 2 * STEP + total.shape[0], LANES), BF16),
        compiler_params=params(),
        name="repack",
    )(left, total)


def spread(x, row=None, lane=None):
    if row is not None:
        x = x[row : row + 1, :]
    if lane is not None:
        x = x[:, lane : lane + 1]
    return jnp.broadcast_to(x, (8, LANES))


def inverse_factor(gram):
    width = 8
    groups = LANES // width
    w = [gram[width * g : width * (g + 1), :] for g in range(groups)]
    row_of = lax.broadcasted_iota(jnp.int32, (width, LANES), 0)
    lane_of = lax.broadcasted_iota(jnp.int32, (width, LANES), 1)
    for g in range(groups):
        first = width * g
        column = {h: [spread(w[h], lane=first + i) for i in range(width)] for h in range(g, groups)}
        inside = (lane_of >= first) & (lane_of < first + width)
        start = jnp.where(inside, jnp.where(lane_of - first == row_of, 1.0, 0.0), w[g])
        y = [spread(start, row=m) for m in range(width)]
        d = [[spread(column[g][i], row=m) for i in range(m + 1)] for m in range(width)]
        low = [[None] * width for _ in range(width)]
        root = [None] * width
        lead = list(column[g + 1]) if g + 1 < groups else None
        for i in range(width):
            if i % 2 == 0:
                first_root = lax.rsqrt(d[i][i])
                det = d[i][i] * d[i + 1][i + 1] - d[i + 1][i] * d[i + 1][i]
                root[i] = first_root
                root[i + 1] = d[i][i] * first_root * lax.rsqrt(det)
            for m in range(i + 1, width):
                low[m][i] = d[m][i] * root[i]
            for m in range(i + 1, width):
                for n in range(i + 1, m + 1):
                    if i % 2 == 1 or m > i + 1:
                        d[m][n] = d[m][n] - low[m][i] * low[n][i]
            y[i] = y[i] * root[i]
            for m in range(i + 1, width):
                y[m] = y[m] - low[m][i] * y[i]
            if lead is not None:
                lead[i] = lead[i] * root[i]
                for m in range(i + 1, width):
                    lead[m] = lead[m] - low[m][i] * lead[i]
        z = [None] * width
        for m in reversed(range(width)):
            value = y[m]
            for k in range(m + 1, width):
                value = value - low[k][m] * z[k]
            z[m] = value * root[m]
        for h in range(g + 1, groups):
            left, right = (lead, y) if h == g + 1 else (column[h], z)
            terms = [left[i] * right[i] for i in range(width)]
            while len(terms) > 1:
                terms = [terms[i] + terms[i + 1] for i in range(0, len(terms), 2)]
            w[h] = jnp.where(inside, 0.0, w[h]) - terms[0]
        rows = y[0]
        for m in range(1, width):
            rows = jnp.where(row_of == m, y[m], rows)
        w[g] = jnp.where(lane_of <= row_of + first, rows, 0.0)
    return jnp.concatenate(w, axis=0)


def basis_kernel(own_ref, other_ref, out_ref):
    half = out_ref.shape[1]

    def left_half(ref):
        parts = [
            ref[piece, :STEP, :].astype(F32) + ref[piece, STEP : 2 * STEP, :].astype(F32)
            for piece in range(half // STEP)
        ]
        return jnp.concatenate(parts, axis=0)

    def product(x, y, dims):
        return lax.dot_general(
            x, y, (dims, ((), ())), precision=lax.Precision.HIGHEST, preferred_element_type=F32
        )

    halves = left_half(own_ref), left_half(other_ref)
    squares = [jnp.sum(p * p, axis=0, keepdims=True) for p in halves]
    scale = lax.rsqrt(squares[0] + squares[1])
    halves = [p * scale for p in halves]
    grams = [product(p, p, ((0,), (0,))) for p in halves]
    inverse = inverse_factor(grams[0] + grams[1])
    for at, p in enumerate(halves):
        out_ref[at] = product(p, inverse, ((1,), (1,))).astype(BF16)


def bases(own, other, half):
    return pl.pallas_call(
        basis_kernel,
        out_shape=jax.ShapeDtypeStruct((2, half, LANES), BF16),
        compiler_params=params(),
        name="basis",
    )(own, other)


def finish_kernel(
    replicas,
    core_ref,
    own_ref,
    other_ref,
    own_sum_ref,
    other_sum_ref,
    basis_ref,
    error_out,
    q_out,
    error_ref,
    q_ref,
    sems,
):
    core = core_ref[0]
    half = basis_ref.shape[1]
    span = own_sum_ref.shape[1] - 2 * STEP

    def slab_of(ref, slab):
        at, end, parts = slab * half, (slab + 1) * half, []
        while at < end:
            piece = at // span
            stop = min(end, (piece + 1) * span)
            parts.append(ref[piece, 2 * STEP + at - piece * span : 2 * STEP + stop - piece * span, :])
            at = stop
        return jnp.concatenate(parts, axis=0)

    def pair_of(read, pair):
        return jnp.concatenate([read(2 * pair), read(2 * pair + 1)], axis=1)

    basis = (basis_ref[0], basis_ref[1])
    flipped = [b.astype(F32).T.astype(BF16) for b in basis]
    copies = []
    for pair in range(q_ref.shape[0] // (2 * LANES)):
        columns = slice(2 * pair * LANES, 2 * (pair + 1) * LANES)
        terms = [
            jnp.dot(flat, pair_of(lambda slab: slab_of(ref, slab), pair), preferred_element_type=F32)
            for flat, ref in zip(flipped, (own_sum_ref, other_sum_ref))
        ]
        scaled = (terms[0] + terms[1]) * (1.0 / replicas)
        q_ref[columns, :] = scaled.T.astype(BF16)
        right = scaled.astype(BF16)
        for which, ref, b in ((core, own_ref, basis[0]), (1 - core, other_ref, basis[1])):
            mine = pair_of(lambda slab: ref[slab * half : (slab + 1) * half, :], pair).astype(F32)
            rows = pl.ds(pl.multiple_of(which * half, half), half)
            error_ref[rows, columns] = (mine - jnp.dot(b, right, preferred_element_type=F32)).astype(BF16)
        copies += [
            pltpu.make_async_copy(q_ref.at[columns, :], q_out.at[columns, :], sems.at[0, pair]),
            pltpu.make_async_copy(error_ref.at[:, columns], error_out.at[:, columns], sems.at[1, pair]),
        ]
        for copy in copies[-2:]:
            copy.start()
    for copy in copies:
        copy.wait()


def finish(core, own, other, own_sum, other_sum, basis, replicas):
    rows, cols = 2 * basis.shape[1], own.shape[0] // basis.shape[1] * LANES
    vmem = pl.BlockSpec(memory_space=pltpu.VMEM)
    return pl.pallas_call(
        lambda *refs: finish_kernel(replicas, *refs),
        out_shape=(jax.ShapeDtypeStruct((rows, cols), BF16), jax.ShapeDtypeStruct((cols, LANES), BF16)),
        in_specs=[pl.BlockSpec(memory_space=pltpu.SMEM)] + [vmem] * 5,
        out_specs=(pl.BlockSpec(memory_space=pl.ANY),) * 2,
        scratch_shapes=[
            pltpu.VMEM((rows, cols), BF16),
            pltpu.VMEM((cols, LANES), BF16),
            pltpu.SemaphoreType.DMA((2, cols // (2 * LANES))),
        ],
        compiler_params=params(),
        name="finish",
    )(core, own, other, own_sum, other_sum, basis)


def on_device(gradient, error, q_prev):
    rows, cols = gradient.shape[1:]
    replicas = lax.axis_size("dp")
    half = rows // 2
    slab_rows = cols // LANES * half
    span = -(-slab_rows // CHIPS // 16) * 16
    core = (lax.axis_index("dp") % 2).astype(jnp.int32).reshape(1)
    twin = [(i, i ^ 1) for i in range(replicas)]
    same_core = [[2 * chip + c for chip in range(CHIPS)] for c in range(2)]

    def across_chips(pieces):
        return lax.all_to_all(pieces, "dp", 0, 0, axis_index_groups=same_core)

    other = half_call(sent_kernel, SENT_LIMIT, core, gradient[0], error[0])
    got = lax.ppermute(other, "dp", twin)
    own, p_own = half_call(kept_kernel, KEPT_LIMIT, core, gradient[0], error[0], q_prev)
    pieces = across_chips(pack(own, got, p_own, q_prev, span))
    left, total = sums(pieces, lax.axis_size("tensor"))
    left = lax.all_to_all(left, "tensor", 0, 0)
    gathered = across_chips(repack(left, total))
    gathered_other = lax.ppermute(gathered, "dp", twin)
    basis = bases(gathered, gathered_other, half)
    new_error, q_next = finish(core, own, other, gathered, gathered_other, basis, replicas)
    return (new_error[None], q_next)


def solution(mesh):
    placed = (P("dp", None, "tensor"), P("dp", None, "tensor"), P("tensor", None))
    return jax.shard_map(
        on_device,
        mesh=mesh,
        in_specs=placed,
        out_specs=(P("dp", None, "tensor"), P("tensor", None)),
        check_vma=False,
    )
```

```python
import jax
import jax.numpy as jnp
from jax import lax
from jax.experimental import pallas as pl
from jax.experimental.pallas import tpu as pltpu
from jax.sharding import PartitionSpec as P

F32, BF16 = jnp.float32, jnp.bfloat16
LANES = 128
CHIPS = 16
MAIN = 160
MIXED = 32
VMEM_LIMIT = 48 * 1024 * 1024
SENT_LIMIT = 52 * 1024 * 1024
KEPT_LIMIT = 52 * 1024 * 1024


def params():
    return pltpu.CompilerParams(vmem_limit_bytes=VMEM_LIMIT)


def combined_half(which, g_in, e_in, out_ref, g_ref, e_ref, sems):
    half, cols = g_ref.shape
    chunks = sems.shape[1]
    count = half // chunks
    copies = []
    for chunk in range(chunks):
        rows = pl.ds(pl.multiple_of(which * half + chunk * count, 16), count)
        here = slice(chunk * count, (chunk + 1) * count)
        pair = [
            pltpu.make_async_copy(g_in.at[rows, :], g_ref.at[here, :], sems.at[0, chunk]),
            pltpu.make_async_copy(e_in.at[rows, :], e_ref.at[here, :], sems.at[1, chunk]),
        ]
        for copy in pair:
            copy.start()
        copies.append(pair)
    for chunk in range(chunks):
        for copy in copies[chunk]:
            copy.wait()
        here = slice(chunk * count, (chunk + 1) * count)
        total = (g_ref[here, :].astype(F32) + e_ref[here, :].astype(F32)).astype(BF16)
        for slab in range(cols // LANES):
            first = slab * half + chunk * count
            out_ref[first : first + count, :] = total[:, slab * LANES : (slab + 1) * LANES]


def sent_kernel(core_ref, g_in, e_in, out_ref, *scratch):
    combined_half(1 - core_ref[0], g_in, e_in, out_ref, *scratch)


def kept_kernel(core_ref, g_in, e_in, q_ref, out_ref, p_ref, *scratch):
    combined_half(core_ref[0], g_in, e_in, out_ref, *scratch)
    p_ref[...] = slab_product(out_ref, q_ref, p_ref.shape[0])


def slab_product(slabs_ref, q_ref, half):
    p = jnp.zeros((half, LANES), F32)
    for pair in range(q_ref.shape[0] // (2 * LANES)):
        two = [slabs_ref[(2 * pair + k) * half : (2 * pair + k + 1) * half, :] for k in range(2)]
        q = q_ref[2 * pair * LANES : 2 * (pair + 1) * LANES, :]
        p += jnp.dot(jnp.concatenate(two, axis=1), q, preferred_element_type=F32)
    return p


def half_call(kernel, limit, core, gradient, error, *more):
    rows, cols = gradient.shape
    half = rows // 2
    chunks = 2
    out = jax.ShapeDtypeStruct((cols // LANES * half, LANES), BF16)
    vmem = pl.BlockSpec(memory_space=pltpu.VMEM)
    anywhere = pl.BlockSpec(memory_space=pl.ANY)
    return pl.pallas_call(
        kernel,
        out_shape=(out, jax.ShapeDtypeStruct((half, LANES), F32)) if more else out,
        in_specs=[pl.BlockSpec(memory_space=pltpu.SMEM), anywhere, anywhere] + [vmem] * len(more),
        out_specs=(vmem, vmem) if more else vmem,
        scratch_shapes=[
            pltpu.VMEM((half, cols), BF16),
            pltpu.VMEM((half, cols), BF16),
            pltpu.SemaphoreType.DMA((2, chunks)),
        ],
        compiler_params=pltpu.CompilerParams(vmem_limit_bytes=limit),
        name="kept" if more else "sent",
    )(core, gradient, error, *more)


def upper_rows():
    return lax.broadcasted_iota(jnp.int32, (8, LANES), 0) < 4


def swap(x):
    return jnp.concatenate([x[4:, :], x[:4, :]], axis=0)


def high_low(x):
    high = x.astype(BF16).astype(F32)
    return high, x - high


def joined(eight, four):
    high, low = high_low(eight)
    high4, low4 = high_low(four)
    return jnp.concatenate([high, low, jnp.where(upper_rows(), high4, low4)], axis=0)


def parted(x):
    return x[:8, :] + x[8:16, :], x[16:, :] + swap(x[16:, :])


def pack_kernel(own_ref, got_ref, p_ref, q_ref, out_ref):
    half = p_ref.shape[0]
    p = p_ref[...] + slab_product(got_ref, q_ref, half)
    for piece in range(CHIPS):
        rows = slice(piece * MAIN, (piece + 1) * MAIN)
        out_ref[piece, :MAIN, :] = (own_ref[rows, :].astype(F32) + got_ref[rows, :].astype(F32)).astype(BF16)
    last = slice(CHIPS * MAIN, CHIPS * (MAIN + 8))
    extra = own_ref[last, :].astype(F32) + got_ref[last, :].astype(F32)
    for piece in range(CHIPS):
        both = p[8 * (CHIPS + piece // 2) : 8 * (CHIPS + piece // 2 + 1), :]
        four = jnp.where(upper_rows() == (piece % 2 == 0), both, swap(both))
        mixed = [extra[8 * piece : 8 * piece + 8, :], joined(p[8 * piece : 8 * piece + 8, :], four)]
        out_ref[piece, MAIN:, :] = jnp.concatenate(mixed, axis=0).astype(BF16)


def pack(own, got, p_own, q_prev):
    return pl.pallas_call(
        pack_kernel,
        out_shape=jax.ShapeDtypeStruct((CHIPS, MAIN + MIXED, LANES), BF16),
        compiler_params=params(),
        name="pack",
    )(own, got, p_own, q_prev)


def sums_kernel(in_ref, left_ref, total_ref):
    total = in_ref[0].astype(F32)
    for chip in range(1, CHIPS):
        total += in_ref[chip].astype(F32)
    left = joined(*parted(total[MAIN + 8 :, :])).astype(BF16)
    for copy in range(left_ref.shape[0]):
        left_ref[copy] = left
    total_ref[...] = total[: MAIN + 8, :]


def sums(pieces, copies):
    return pl.pallas_call(
        sums_kernel,
        out_shape=(
            jax.ShapeDtypeStruct((copies, MIXED - 8, LANES), BF16),
            jax.ShapeDtypeStruct((MAIN + 8, LANES), F32),
        ),
        compiler_params=params(),
        name="sums",
    )(pieces)


def repack_kernel(left_ref, total_ref, out_ref):
    left = left_ref[0].astype(F32)
    for at in range(1, left_ref.shape[0]):
        left += left_ref[at].astype(F32)
    piece = jnp.concatenate([total_ref[...], joined(*parted(left))], axis=0).astype(BF16)
    for chip in range(CHIPS):
        out_ref[chip] = piece


def repack(left, total):
    return pl.pallas_call(
        repack_kernel,
        out_shape=jax.ShapeDtypeStruct((CHIPS, MAIN + MIXED, LANES), BF16),
        compiler_params=params(),
        name="repack",
    )(left, total)


def spread(x, row=None, lane=None):
    if row is not None:
        x = x[row : row + 1, :]
    if lane is not None:
        x = x[:, lane : lane + 1]
    return jnp.broadcast_to(x, (8, LANES))


def inverse_factor(gram):
    width = 8
    groups = LANES // width
    w = [gram[width * g : width * (g + 1), :] for g in range(groups)]
    row_of = lax.broadcasted_iota(jnp.int32, (width, LANES), 0)
    lane_of = lax.broadcasted_iota(jnp.int32, (width, LANES), 1)
    for g in range(groups):
        first = width * g
        column = {h: [spread(w[h], lane=first + i) for i in range(width)] for h in range(g, groups)}
        inside = (lane_of >= first) & (lane_of < first + width)
        start = jnp.where(inside, jnp.where(lane_of - first == row_of, 1.0, 0.0), w[g])
        y = [spread(start, row=m) for m in range(width)]
        d = [[spread(column[g][i], row=m) for i in range(m + 1)] for m in range(width)]
        low = [[None] * width for _ in range(width)]
        root = [None] * width
        lead = list(column[g + 1]) if g + 1 < groups else None
        for i in range(width):
            if i % 2 == 0:
                first_root = lax.rsqrt(d[i][i])
                det = d[i][i] * d[i + 1][i + 1] - d[i + 1][i] * d[i + 1][i]
                root[i] = first_root
                root[i + 1] = d[i][i] * first_root * lax.rsqrt(det)
            for m in range(i + 1, width):
                low[m][i] = d[m][i] * root[i]
            for m in range(i + 1, width):
                for n in range(i + 1, m + 1):
                    if i % 2 == 1 or m > i + 1:
                        d[m][n] = d[m][n] - low[m][i] * low[n][i]
            y[i] = y[i] * root[i]
            for m in range(i + 1, width):
                y[m] = y[m] - low[m][i] * y[i]
            if lead is not None:
                lead[i] = lead[i] * root[i]
                for m in range(i + 1, width):
                    lead[m] = lead[m] - low[m][i] * lead[i]
        z = [None] * width
        for m in reversed(range(width)):
            value = y[m]
            for k in range(m + 1, width):
                value = value - low[k][m] * z[k]
            z[m] = value * root[m]
        for h in range(g + 1, groups):
            left, right = (lead, y) if h == g + 1 else (column[h], z)
            terms = [left[i] * right[i] for i in range(width)]
            while len(terms) > 1:
                terms = [terms[i] + terms[i + 1] for i in range(0, len(terms), 2)]
            w[h] = jnp.where(inside, 0.0, w[h]) - terms[0]
        rows = y[0]
        for m in range(1, width):
            rows = jnp.where(row_of == m, y[m], rows)
        w[g] = jnp.where(lane_of <= row_of + first, rows, 0.0)
    return jnp.concatenate(w, axis=0)


def basis_kernel(own_ref, other_ref, out_ref):
    half = out_ref.shape[1]

    def left_half(ref):
        parts = [parted(ref[piece, MAIN:, :].astype(F32)[8:, :]) for piece in range(CHIPS)]
        lower = [jnp.where(upper_rows(), parts[2 * k][1], parts[2 * k + 1][1]) for k in range(CHIPS // 2)]
        return jnp.concatenate([eight for eight, _ in parts] + lower, axis=0)

    def product(x, y, dims):
        return lax.dot_general(
            x, y, (dims, ((), ())), precision=lax.Precision.HIGHEST, preferred_element_type=F32
        )

    halves = left_half(own_ref), left_half(other_ref)
    squares = [jnp.sum(p * p, axis=0, keepdims=True) for p in halves]
    scale = lax.rsqrt(squares[0] + squares[1])
    halves = [p * scale for p in halves]
    grams = [product(p, p, ((0,), (0,))) for p in halves]
    inverse = inverse_factor(grams[0] + grams[1])
    for at, p in enumerate(halves):
        out_ref[at] = product(p, inverse, ((1,), (1,))).astype(BF16)


def bases(own, other, half):
    return pl.pallas_call(
        basis_kernel,
        out_shape=jax.ShapeDtypeStruct((2, half, LANES), BF16),
        compiler_params=params(),
        name="basis",
    )(own, other)


def finish_kernel(
    replicas,
    core_ref,
    own_ref,
    other_ref,
    own_sum_ref,
    other_sum_ref,
    basis_ref,
    error_out,
    q_out,
    error_ref,
    q_ref,
    sems,
):
    core = core_ref[0]
    half = basis_ref.shape[1]

    def slab_of(ref, slab):
        at, end, parts = slab * half, (slab + 1) * half, []
        while at < min(end, CHIPS * MAIN):
            piece = at // MAIN
            stop = min(end, (piece + 1) * MAIN)
            parts.append(ref[piece, at - piece * MAIN : stop - piece * MAIN, :])
            at = stop
        if at < end:
            extra = [ref[piece, MAIN : MAIN + 16, :].astype(F32)[:8, :] for piece in range(CHIPS)]
            parts.append(jnp.concatenate(extra, axis=0).astype(BF16))
        return jnp.concatenate(parts, axis=0)

    def pair_of(read, pair):
        return jnp.concatenate([read(2 * pair), read(2 * pair + 1)], axis=1)

    basis = (basis_ref[0], basis_ref[1])
    flipped = [b.astype(F32).T.astype(BF16) for b in basis]
    copies = []
    for pair in range(q_ref.shape[0] // (2 * LANES)):
        columns = slice(2 * pair * LANES, 2 * (pair + 1) * LANES)
        terms = [
            jnp.dot(flat, pair_of(lambda slab: slab_of(ref, slab), pair), preferred_element_type=F32)
            for flat, ref in zip(flipped, (own_sum_ref, other_sum_ref))
        ]
        scaled = (terms[0] + terms[1]) * (1.0 / replicas)
        q_ref[columns, :] = scaled.T.astype(BF16)
        right = scaled.astype(BF16)
        for which, ref, b in ((core, own_ref, basis[0]), (1 - core, other_ref, basis[1])):
            mine = pair_of(lambda slab: ref[slab * half : (slab + 1) * half, :], pair).astype(F32)
            rows = pl.ds(pl.multiple_of(which * half, half), half)
            error_ref[rows, columns] = (mine - jnp.dot(b, right, preferred_element_type=F32)).astype(BF16)
        copies += [
            pltpu.make_async_copy(q_ref.at[columns, :], q_out.at[columns, :], sems.at[0, pair]),
            pltpu.make_async_copy(error_ref.at[:, columns], error_out.at[:, columns], sems.at[1, pair]),
        ]
        for copy in copies[-2:]:
            copy.start()
    for copy in copies:
        copy.wait()


def finish(core, own, other, own_sum, other_sum, basis, replicas):
    rows, cols = 2 * basis.shape[1], own.shape[0] // basis.shape[1] * LANES
    vmem = pl.BlockSpec(memory_space=pltpu.VMEM)
    return pl.pallas_call(
        lambda *refs: finish_kernel(replicas, *refs),
        out_shape=(jax.ShapeDtypeStruct((rows, cols), BF16), jax.ShapeDtypeStruct((cols, LANES), BF16)),
        in_specs=[pl.BlockSpec(memory_space=pltpu.SMEM)] + [vmem] * 5,
        out_specs=(pl.BlockSpec(memory_space=pl.ANY),) * 2,
        scratch_shapes=[
            pltpu.VMEM((rows, cols), BF16),
            pltpu.VMEM((cols, LANES), BF16),
            pltpu.SemaphoreType.DMA((2, cols // (2 * LANES))),
        ],
        compiler_params=params(),
        name="finish",
    )(core, own, other, own_sum, other_sum, basis)


def on_device(gradient, error, q_prev):
    rows, cols = gradient.shape[1:]
    replicas = lax.axis_size("dp")
    half = rows // 2
    core = (lax.axis_index("dp") % 2).astype(jnp.int32).reshape(1)
    twin = [(i, i ^ 1) for i in range(replicas)]
    same_core = [[2 * chip + c for chip in range(CHIPS)] for c in range(2)]

    def across_chips(pieces):
        return lax.all_to_all(pieces, "dp", 0, 0, axis_index_groups=same_core)

    other = half_call(sent_kernel, SENT_LIMIT, core, gradient[0], error[0])
    got = lax.ppermute(other, "dp", twin)
    own, p_own = half_call(kept_kernel, KEPT_LIMIT, core, gradient[0], error[0], q_prev)
    pieces = across_chips(pack(own, got, p_own, q_prev))
    left, total = sums(pieces, lax.axis_size("tensor"))
    left = lax.all_to_all(left, "tensor", 0, 0)
    gathered = across_chips(repack(left, total))
    gathered_other = lax.ppermute(gathered, "dp", twin)
    basis = bases(gathered, gathered_other, half)
    new_error, q_next = finish(core, own, other, gathered, gathered_other, basis, replicas)
    return (new_error[None], q_next)


def solution(mesh):
    placed = (P("dp", None, "tensor"), P("dp", None, "tensor"), P("tensor", None))
    return jax.shard_map(
        on_device,
        mesh=mesh,
        in_specs=placed,
        out_specs=(P("dp", None, "tensor"), P("tensor", None)),
        check_vma=False,
    )
```

```python
import jax
import jax.numpy as jnp
from jax import lax
from jax.experimental import pallas as pl
from jax.experimental.pallas import tpu as pltpu
from jax.sharding import PartitionSpec as P

F32, BF16 = jnp.float32, jnp.bfloat16
LANES = 128
CHIPS = 16
MAIN = 160
MIXED = 32
VMEM_LIMIT = 48 * 1024 * 1024
SENT_LIMIT = 52 * 1024 * 1024
KEPT_LIMIT = 52 * 1024 * 1024


def params():
    return pltpu.CompilerParams(vmem_limit_bytes=VMEM_LIMIT)


def combined_half(which, g_in, e_in, out_ref, g_ref, e_ref, sems):
    half, cols = g_ref.shape
    chunks = sems.shape[1]
    count = half // chunks
    copies = []
    for chunk in range(chunks):
        rows = pl.ds(pl.multiple_of(which * half + chunk * count, 16), count)
        here = slice(chunk * count, (chunk + 1) * count)
        pair = [
            pltpu.make_async_copy(g_in.at[rows, :], g_ref.at[here, :], sems.at[0, chunk]),
            pltpu.make_async_copy(e_in.at[rows, :], e_ref.at[here, :], sems.at[1, chunk]),
        ]
        for copy in pair:
            copy.start()
        copies.append(pair)
    for chunk in range(chunks):
        for copy in copies[chunk]:
            copy.wait()
        here = slice(chunk * count, (chunk + 1) * count)
        total = (g_ref[here, :].astype(F32) + e_ref[here, :].astype(F32)).astype(BF16)
        for slab in range(cols // LANES):
            first = slab * half + chunk * count
            out_ref[first : first + count, :] = total[:, slab * LANES : (slab + 1) * LANES]


def sent_kernel(core_ref, g_in, e_in, out_ref, *scratch):
    combined_half(1 - core_ref[0], g_in, e_in, out_ref, *scratch)


def kept_kernel(core_ref, g_in, e_in, q_ref, out_ref, p_ref, *scratch):
    combined_half(core_ref[0], g_in, e_in, out_ref, *scratch)
    p_ref[...] = slab_product(out_ref, q_ref, p_ref.shape[0])


def slab_product(slabs_ref, q_ref, half):
    p = jnp.zeros((half, LANES), F32)
    for pair in range(q_ref.shape[0] // (2 * LANES)):
        two = [slabs_ref[(2 * pair + k) * half : (2 * pair + k + 1) * half, :] for k in range(2)]
        q = q_ref[2 * pair * LANES : 2 * (pair + 1) * LANES, :]
        p += jnp.dot(jnp.concatenate(two, axis=1), q, preferred_element_type=F32)
    return p


def half_call(kernel, limit, core, gradient, error, *more):
    rows, cols = gradient.shape
    half = rows // 2
    chunks = 2
    out = jax.ShapeDtypeStruct((cols // LANES * half, LANES), BF16)
    vmem = pl.BlockSpec(memory_space=pltpu.VMEM)
    anywhere = pl.BlockSpec(memory_space=pl.ANY)
    return pl.pallas_call(
        kernel,
        out_shape=(out, jax.ShapeDtypeStruct((half, LANES), F32)) if more else out,
        in_specs=[pl.BlockSpec(memory_space=pltpu.SMEM), anywhere, anywhere] + [vmem] * len(more),
        out_specs=(vmem, vmem) if more else vmem,
        scratch_shapes=[
            pltpu.VMEM((half, cols), BF16),
            pltpu.VMEM((half, cols), BF16),
            pltpu.SemaphoreType.DMA((2, chunks)),
        ],
        compiler_params=pltpu.CompilerParams(vmem_limit_bytes=limit),
        name="kept" if more else "sent",
    )(core, gradient, error, *more)


def upper_rows():
    return lax.broadcasted_iota(jnp.int32, (8, LANES), 0) < 4


def swap(x):
    return jnp.concatenate([x[4:, :], x[:4, :]], axis=0)


def high_low(x):
    high = x.astype(BF16).astype(F32)
    return high, x - high


def joined(eight, four):
    high, low = high_low(eight)
    high4, low4 = high_low(four)
    return jnp.concatenate([high, low, jnp.where(upper_rows(), high4, low4)], axis=0)


def parted(x):
    return x[:8, :] + x[8:16, :], x[16:, :] + swap(x[16:, :])


def pack_kernel(own_ref, got_ref, p_ref, q_ref, out_ref):
    half = p_ref.shape[0]
    p = p_ref[...] + slab_product(got_ref, q_ref, half)
    for piece in range(CHIPS):
        rows = slice(piece * MAIN, (piece + 1) * MAIN)
        out_ref[piece, :MAIN, :] = (own_ref[rows, :].astype(F32) + got_ref[rows, :].astype(F32)).astype(BF16)
    last = slice(CHIPS * MAIN, CHIPS * (MAIN + 8))
    extra = own_ref[last, :].astype(F32) + got_ref[last, :].astype(F32)
    for piece in range(CHIPS):
        both = p[8 * (CHIPS + piece // 2) : 8 * (CHIPS + piece // 2 + 1), :]
        four = jnp.where(upper_rows() == (piece % 2 == 0), both, swap(both))
        mixed = [extra[8 * piece : 8 * piece + 8, :], joined(p[8 * piece : 8 * piece + 8, :], four)]
        out_ref[piece, MAIN:, :] = jnp.concatenate(mixed, axis=0).astype(BF16)


def pack(own, got, p_own, q_prev):
    return pl.pallas_call(
        pack_kernel,
        out_shape=jax.ShapeDtypeStruct((CHIPS, MAIN + MIXED, LANES), BF16),
        compiler_params=params(),
        name="pack",
    )(own, got, p_own, q_prev)


def sums_kernel(in_ref, left_ref, total_ref):
    total = in_ref[0].astype(F32)
    for chip in range(1, CHIPS):
        total += in_ref[chip].astype(F32)
    left = joined(*parted(total[MAIN + 8 :, :])).astype(BF16)
    for copy in range(left_ref.shape[0]):
        left_ref[copy] = left
    total_ref[...] = total[: MAIN + 8, :]


def sums(pieces, copies):
    return pl.pallas_call(
        sums_kernel,
        out_shape=(
            jax.ShapeDtypeStruct((copies, MIXED - 8, LANES), BF16),
            jax.ShapeDtypeStruct((MAIN + 8, LANES), F32),
        ),
        compiler_params=params(),
        name="sums",
    )(pieces)


def repack_kernel(left_ref, total_ref, out_ref):
    left = left_ref[0].astype(F32)
    for at in range(1, left_ref.shape[0]):
        left += left_ref[at].astype(F32)
    piece = jnp.concatenate([total_ref[...], joined(*parted(left))], axis=0).astype(BF16)
    for chip in range(CHIPS):
        out_ref[chip] = piece


def repack(left, total):
    return pl.pallas_call(
        repack_kernel,
        out_shape=jax.ShapeDtypeStruct((CHIPS, MAIN + MIXED, LANES), BF16),
        compiler_params=params(),
        name="repack",
    )(left, total)


def spread(x, row=None, lane=None):
    if row is not None:
        x = x[row : row + 1, :]
    if lane is not None:
        x = x[:, lane : lane + 1]
    return jnp.broadcast_to(x, (8, LANES))


def added(terms):
    while len(terms) > 1:
        terms = [terms[i] + terms[i + 1] for i in range(0, len(terms), 2)]
    return terms[0]


def inverse_factor(gram):
    width = 8
    groups = LANES // width
    w = [gram[width * g : width * (g + 1), :] for g in range(groups)]
    row_of = lax.broadcasted_iota(jnp.int32, (width, LANES), 0)
    lane_of = lax.broadcasted_iota(jnp.int32, (width, LANES), 1)
    pivots = [spread(w[0], lane=i) for i in range(width)]
    for g in range(groups):
        first = width * g
        more = g + 1 < groups
        column = {h: [spread(w[h], lane=first + i) for i in range(width)] for h in range(g + 1, groups)}
        ahead = [spread(w[g + 1], lane=first + width + n) for n in range(width)] if more else []
        inside = (lane_of >= first) & (lane_of < first + width)
        start = jnp.where(inside, jnp.where(lane_of - first == row_of, 1.0, 0.0), w[g])
        y = [spread(start, row=m) for m in range(width)]
        d = [[spread(pivots[i], row=m) for i in range(m + 1)] for m in range(width)]
        low = [[None] * width for _ in range(width)]
        root = [None] * width
        lead = list(column[g + 1]) if more else None
        for i in range(width):
            if i % 2 == 0:
                first_root = lax.rsqrt(d[i][i])
                det = d[i][i] * d[i + 1][i + 1] - d[i + 1][i] * d[i + 1][i]
                root[i] = first_root
                root[i + 1] = d[i][i] * first_root * lax.rsqrt(det)
            for m in range(i + 1, width):
                low[m][i] = d[m][i] * root[i]
            for m in range(i + 1, width):
                for n in range(i + 1, m + 1):
                    if i % 2 == 1 or m > i + 1:
                        d[m][n] = d[m][n] - low[m][i] * low[n][i]
            y[i] = y[i] * root[i]
            for m in range(i + 1, width):
                y[m] = y[m] - low[m][i] * y[i]
            if more:
                lead[i] = lead[i] * root[i]
                for m in range(i + 1, width):
                    lead[m] = lead[m] - low[m][i] * lead[i]
        z = [None] * width
        for m in reversed(range(width)):
            value = y[m]
            for k in range(m + 1, width):
                value = value - low[k][m] * z[k]
            z[m] = value * root[m]
        for h in range(g + 1, groups):
            left, right = (lead, y) if h == g + 1 else (column[h], z)
            w[h] = jnp.where(inside, 0.0, w[h]) - added([left[i] * right[i] for i in range(width)])
        pivots = [
            ahead[n] - added([lead[i] * spread(lead[i], row=n) for i in range(width)]) for n in range(len(ahead))
        ]
        rows = y[0]
        for m in range(1, width):
            rows = jnp.where(row_of == m, y[m], rows)
        w[g] = jnp.where(lane_of <= row_of + first, rows, 0.0)
    return jnp.concatenate(w, axis=0)


def basis_kernel(core_ref, own_ref, other_ref, out_ref):
    def left_half(ref):
        parts = [parted(ref[piece, MAIN:, :].astype(F32)[8:, :]) for piece in range(CHIPS)]
        lower = [jnp.where(upper_rows(), parts[2 * k][1], parts[2 * k + 1][1]) for k in range(CHIPS // 2)]
        return jnp.concatenate([eight for eight, _ in parts] + lower, axis=0)

    def product(x, y, dims):
        return lax.dot_general(
            x, y, (dims, ((), ())), precision=lax.Precision.HIGHEST, preferred_element_type=F32
        )

    half = out_ref.shape[1]
    own, other = left_half(own_ref), left_half(other_ref)
    is_first = core_ref[0] == 0
    p = jnp.concatenate([jnp.where(is_first, own, other), jnp.where(is_first, other, own)], axis=0)
    p = p * lax.rsqrt(jnp.sum(p * p, axis=0, keepdims=True))
    inverse = inverse_factor(product(p, p, ((0,), (0,))))
    basis = product(p, inverse, ((1,), (1,))).astype(BF16)
    out_ref[0] = basis[:half, :]
    out_ref[1] = basis[half:, :]


def bases(core, own, other, half):
    vmem = pl.BlockSpec(memory_space=pltpu.VMEM)
    return pl.pallas_call(
        basis_kernel,
        out_shape=jax.ShapeDtypeStruct((2, half, LANES), BF16),
        in_specs=[pl.BlockSpec(memory_space=pltpu.SMEM), vmem, vmem],
        out_specs=vmem,
        compiler_params=params(),
        name="basis",
    )(core, own, other)


def finish_kernel(
    replicas,
    core_ref,
    own_ref,
    other_ref,
    own_sum_ref,
    other_sum_ref,
    basis_ref,
    error_out,
    q_out,
    error_ref,
    q_ref,
    sems,
):
    core = core_ref[0]
    half = basis_ref.shape[1]

    def slab_of(ref, slab):
        at, end, parts = slab * half, (slab + 1) * half, []
        while at < min(end, CHIPS * MAIN):
            piece = at // MAIN
            stop = min(end, (piece + 1) * MAIN)
            parts.append(ref[piece, at - piece * MAIN : stop - piece * MAIN, :])
            at = stop
        if at < end:
            extra = [ref[piece, MAIN : MAIN + 16, :].astype(F32)[:8, :] for piece in range(CHIPS)]
            parts.append(jnp.concatenate(extra, axis=0).astype(BF16))
        return jnp.concatenate(parts, axis=0)

    def pair_of(read, pair):
        return jnp.concatenate([read(2 * pair), read(2 * pair + 1)], axis=1)

    basis = (basis_ref[core], basis_ref[1 - core])
    flipped = [b.astype(F32).T.astype(BF16) for b in basis]
    copies = []
    for pair in range(q_ref.shape[0] // (2 * LANES)):
        columns = slice(2 * pair * LANES, 2 * (pair + 1) * LANES)
        terms = [
            jnp.dot(flat, pair_of(lambda slab: slab_of(ref, slab), pair), preferred_element_type=F32)
            for flat, ref in zip(flipped, (own_sum_ref, other_sum_ref))
        ]
        scaled = (terms[0] + terms[1]) * (1.0 / replicas)
        q_ref[columns, :] = scaled.T.astype(BF16)
        right = scaled.astype(BF16)
        for at, (which, ref, b) in enumerate(((core, own_ref, basis[0]), (1 - core, other_ref, basis[1]))):
            mine = pair_of(lambda slab: ref[slab * half : (slab + 1) * half, :], pair).astype(F32)
            rows = pl.ds(pl.multiple_of(which * half, half), half)
            error_ref[rows, columns] = (mine - jnp.dot(b, right, preferred_element_type=F32)).astype(BF16)
            copies.append(
                pltpu.make_async_copy(error_ref.at[rows, columns], error_out.at[rows, columns], sems.at[at, pair])
            )
            copies[-1].start()
        copies.append(pltpu.make_async_copy(q_ref.at[columns, :], q_out.at[columns, :], sems.at[2, pair]))
        copies[-1].start()
    for copy in copies:
        copy.wait()


def finish(core, own, other, own_sum, other_sum, basis, replicas):
    rows, cols = 2 * basis.shape[1], own.shape[0] // basis.shape[1] * LANES
    vmem = pl.BlockSpec(memory_space=pltpu.VMEM)
    return pl.pallas_call(
        lambda *refs: finish_kernel(replicas, *refs),
        out_shape=(jax.ShapeDtypeStruct((rows, cols), BF16), jax.ShapeDtypeStruct((cols, LANES), BF16)),
        in_specs=[pl.BlockSpec(memory_space=pltpu.SMEM)] + [vmem] * 5,
        out_specs=(pl.BlockSpec(memory_space=pl.ANY),) * 2,
        scratch_shapes=[
            pltpu.VMEM((rows, cols), BF16),
            pltpu.VMEM((cols, LANES), BF16),
            pltpu.SemaphoreType.DMA((3, cols // (2 * LANES))),
        ],
        compiler_params=params(),
        name="finish",
    )(core, own, other, own_sum, other_sum, basis)


def on_device(gradient, error, q_prev):
    rows, cols = gradient.shape[1:]
    replicas = lax.axis_size("dp")
    half = rows // 2
    core = (lax.axis_index("dp") % 2).astype(jnp.int32).reshape(1)
    twin = [(i, i ^ 1) for i in range(replicas)]
    same_core = [[2 * chip + c for chip in range(CHIPS)] for c in range(2)]

    def across_chips(pieces):
        return lax.all_to_all(pieces, "dp", 0, 0, axis_index_groups=same_core)

    other = half_call(sent_kernel, SENT_LIMIT, core, gradient[0], error[0])
    got = lax.ppermute(other, "dp", twin)
    own, p_own = half_call(kept_kernel, KEPT_LIMIT, core, gradient[0], error[0], q_prev)
    pieces = across_chips(pack(own, got, p_own, q_prev))
    left, total = sums(pieces, lax.axis_size("tensor"))
    left = lax.all_to_all(left, "tensor", 0, 0)
    gathered = across_chips(repack(left, total))
    gathered_other = lax.ppermute(gathered, "dp", twin)
    basis = bases(core, gathered, gathered_other, half)
    new_error, q_next = finish(core, own, other, gathered, gathered_other, basis, replicas)
    return (new_error[None], q_next)


def solution(mesh):
    placed = (P("dp", None, "tensor"), P("dp", None, "tensor"), P("tensor", None))
    return jax.shard_map(
        on_device,
        mesh=mesh,
        in_specs=placed,
        out_specs=(P("dp", None, "tensor"), P("tensor", None)),
        check_vma=False,
    )
```

```python
import jax
import jax.numpy as jnp
from jax import lax
from jax.experimental import pallas as pl
from jax.experimental.pallas import tpu as pltpu
from jax.sharding import PartitionSpec as P

F32, BF16 = jnp.float32, jnp.bfloat16
LANES = 128
CHIPS = 16
MAIN = 160
MIXED = 32
VMEM_LIMIT = 48 * 1024 * 1024
SENT_LIMIT = 52 * 1024 * 1024
KEPT_LIMIT = 52 * 1024 * 1024


def params():
    return pltpu.CompilerParams(vmem_limit_bytes=VMEM_LIMIT)


def combined_half(which, g_in, e_in, out_ref, g_ref, e_ref, sems):
    half, cols = g_ref.shape
    chunks = sems.shape[1]
    count = half // chunks
    copies = []
    for chunk in range(chunks):
        rows = pl.ds(pl.multiple_of(which * half + chunk * count, 16), count)
        here = slice(chunk * count, (chunk + 1) * count)
        pair = [
            pltpu.make_async_copy(g_in.at[rows, :], g_ref.at[here, :], sems.at[0, chunk]),
            pltpu.make_async_copy(e_in.at[rows, :], e_ref.at[here, :], sems.at[1, chunk]),
        ]
        for copy in pair:
            copy.start()
        copies.append(pair)
    for chunk in range(chunks):
        for copy in copies[chunk]:
            copy.wait()
        here = slice(chunk * count, (chunk + 1) * count)
        total = (g_ref[here, :].astype(F32) + e_ref[here, :].astype(F32)).astype(BF16)
        for slab in range(cols // LANES):
            first = slab * half + chunk * count
            out_ref[first : first + count, :] = total[:, slab * LANES : (slab + 1) * LANES]


def sent_kernel(core_ref, g_in, e_in, out_ref, *scratch):
    combined_half(1 - core_ref[0], g_in, e_in, out_ref, *scratch)


def kept_kernel(core_ref, g_in, e_in, q_ref, out_ref, p_ref, *scratch):
    combined_half(core_ref[0], g_in, e_in, out_ref, *scratch)
    p_ref[...] = slab_product(out_ref, q_ref, p_ref.shape[0])


def slab_product(slabs_ref, q_ref, half):
    p = jnp.zeros((half, LANES), F32)
    for pair in range(q_ref.shape[0] // (2 * LANES)):
        two = [slabs_ref[(2 * pair + k) * half : (2 * pair + k + 1) * half, :] for k in range(2)]
        q = q_ref[2 * pair * LANES : 2 * (pair + 1) * LANES, :]
        p += jnp.dot(jnp.concatenate(two, axis=1), q, preferred_element_type=F32)
    return p


def half_call(kernel, limit, core, gradient, error, *more):
    rows, cols = gradient.shape
    half = rows // 2
    chunks = 2
    out = jax.ShapeDtypeStruct((cols // LANES * half, LANES), BF16)
    vmem = pl.BlockSpec(memory_space=pltpu.VMEM)
    anywhere = pl.BlockSpec(memory_space=pl.ANY)
    return pl.pallas_call(
        kernel,
        out_shape=(out, jax.ShapeDtypeStruct((half, LANES), F32)) if more else out,
        in_specs=[pl.BlockSpec(memory_space=pltpu.SMEM), anywhere, anywhere] + [vmem] * len(more),
        out_specs=(vmem, vmem) if more else vmem,
        scratch_shapes=[
            pltpu.VMEM((half, cols), BF16),
            pltpu.VMEM((half, cols), BF16),
            pltpu.SemaphoreType.DMA((2, chunks)),
        ],
        compiler_params=pltpu.CompilerParams(vmem_limit_bytes=limit),
        name="kept" if more else "sent",
    )(core, gradient, error, *more)


def upper_rows():
    return lax.broadcasted_iota(jnp.int32, (8, LANES), 0) < 4


def swap(x):
    return jnp.concatenate([x[4:, :], x[:4, :]], axis=0)


def high_low(x):
    high = x.astype(BF16).astype(F32)
    return high, x - high


def joined(eight, four):
    high, low = high_low(eight)
    high4, low4 = high_low(four)
    return jnp.concatenate([high, low, jnp.where(upper_rows(), high4, low4)], axis=0)


def parted(x):
    return x[:8, :] + x[8:16, :], x[16:, :] + swap(x[16:, :])


def pack_kernel(own_ref, got_ref, p_ref, q_ref, out_ref):
    half = p_ref.shape[0]
    p = p_ref[...] + slab_product(got_ref, q_ref, half)
    for piece in range(CHIPS):
        rows = slice(piece * MAIN, (piece + 1) * MAIN)
        out_ref[piece, :MAIN, :] = (own_ref[rows, :].astype(F32) + got_ref[rows, :].astype(F32)).astype(BF16)
    last = slice(CHIPS * MAIN, CHIPS * (MAIN + 8))
    extra = own_ref[last, :].astype(F32) + got_ref[last, :].astype(F32)
    for piece in range(CHIPS):
        both = p[8 * (CHIPS + piece // 2) : 8 * (CHIPS + piece // 2 + 1), :]
        four = jnp.where(upper_rows() == (piece % 2 == 0), both, swap(both))
        mixed = [extra[8 * piece : 8 * piece + 8, :], joined(p[8 * piece : 8 * piece + 8, :], four)]
        out_ref[piece, MAIN:, :] = jnp.concatenate(mixed, axis=0).astype(BF16)


def pack(own, got, p_own, q_prev):
    return pl.pallas_call(
        pack_kernel,
        out_shape=jax.ShapeDtypeStruct((CHIPS, MAIN + MIXED, LANES), BF16),
        compiler_params=params(),
        name="pack",
    )(own, got, p_own, q_prev)


def sums_kernel(in_ref, left_ref, total_ref):
    total = in_ref[0].astype(F32)
    for chip in range(1, CHIPS):
        total += in_ref[chip].astype(F32)
    left = joined(*parted(total[MAIN + 8 :, :])).astype(BF16)
    for copy in range(left_ref.shape[0]):
        left_ref[copy] = left
    total_ref[...] = total[: MAIN + 8, :]


def sums(pieces, copies):
    return pl.pallas_call(
        sums_kernel,
        out_shape=(
            jax.ShapeDtypeStruct((copies, MIXED - 8, LANES), BF16),
            jax.ShapeDtypeStruct((MAIN + 8, LANES), F32),
        ),
        compiler_params=params(),
        name="sums",
    )(pieces)


def repack_kernel(left_ref, total_ref, out_ref):
    left = left_ref[0].astype(F32)
    for at in range(1, left_ref.shape[0]):
        left += left_ref[at].astype(F32)
    piece = jnp.concatenate([total_ref[...], joined(*parted(left))], axis=0).astype(BF16)
    for chip in range(CHIPS):
        out_ref[chip] = piece


def repack(left, total):
    return pl.pallas_call(
        repack_kernel,
        out_shape=jax.ShapeDtypeStruct((CHIPS, MAIN + MIXED, LANES), BF16),
        compiler_params=params(),
        name="repack",
    )(left, total)


def spread(x, row=None, lane=None):
    if row is not None:
        x = x[row : row + 1, :]
    if lane is not None:
        x = x[:, lane : lane + 1]
    return jnp.broadcast_to(x, (8, LANES))


def added(terms):
    while len(terms) > 1:
        terms = [terms[i] + terms[i + 1] for i in range(0, len(terms), 2)]
    return terms[0]


def inverse_factor(gram):
    width = 8
    groups = LANES // width
    w = [gram[width * g : width * (g + 1), :] for g in range(groups)]
    row_of = lax.broadcasted_iota(jnp.int32, (width, LANES), 0)
    lane_of = lax.broadcasted_iota(jnp.int32, (width, LANES), 1)
    pivots = [spread(w[0], lane=i) for i in range(width)]
    for g in range(groups):
        first = width * g
        more = g + 1 < groups
        column = {h: [spread(w[h], lane=first + i) for i in range(width)] for h in range(g + 1, groups)}
        ahead = [spread(w[g + 1], lane=first + width + n) for n in range(width)] if more else []
        inside = (lane_of >= first) & (lane_of < first + width)
        start = jnp.where(inside, jnp.where(lane_of - first == row_of, 1.0, 0.0), w[g])
        y = [spread(start, row=m) for m in range(width)]
        d = [[spread(pivots[i], row=m) for i in range(m + 1)] for m in range(width)]
        low = [[None] * width for _ in range(width)]
        root = [None] * width
        lead = list(column[g + 1]) if more else None
        for i in range(width):
            if i % 2 == 0:
                first_root = lax.rsqrt(d[i][i])
                det = d[i][i] * d[i + 1][i + 1] - d[i + 1][i] * d[i + 1][i]
                root[i] = first_root
                root[i + 1] = d[i][i] * first_root * lax.rsqrt(det)
            for m in range(i + 1, width):
                low[m][i] = d[m][i] * root[i]
            for m in range(i + 1, width):
                for n in range(i + 1, m + 1):
                    if i % 2 == 1 or m > i + 1:
                        d[m][n] = d[m][n] - low[m][i] * low[n][i]
            y[i] = y[i] * root[i]
            for m in range(i + 1, width):
                y[m] = y[m] - low[m][i] * y[i]
            if more:
                lead[i] = lead[i] * root[i]
                for m in range(i + 1, width):
                    lead[m] = lead[m] - low[m][i] * lead[i]
        z = [None] * width
        for m in reversed(range(width)):
            value = y[m]
            for k in range(m + 1, width):
                value = value - low[k][m] * z[k]
            z[m] = value * root[m]
        for h in range(g + 1, groups):
            left, right = (lead, y) if h == g + 1 else (column[h], z)
            w[h] = jnp.where(inside, 0.0, w[h]) - added([left[i] * right[i] for i in range(width)])
        pivots = [
            ahead[n] - added([lead[i] * spread(lead[i], row=n) for i in range(width)]) for n in range(len(ahead))
        ]
        rows = y[0]
        for m in range(1, width):
            rows = jnp.where(row_of == m, y[m], rows)
        w[g] = jnp.where(lane_of <= row_of + first, rows, 0.0)
    return jnp.concatenate(w, axis=0)


def basis_kernel(core_ref, own_ref, other_ref, out_ref):
    def left_half(ref):
        parts = [parted(ref[piece, MAIN:, :].astype(F32)[8:, :]) for piece in range(CHIPS)]
        lower = [jnp.where(upper_rows(), parts[2 * k][1], parts[2 * k + 1][1]) for k in range(CHIPS // 2)]
        return jnp.concatenate([eight for eight, _ in parts] + lower, axis=0)

    def product(x, y, dims):
        return lax.dot_general(
            x, y, (dims, ((), ())), precision=lax.Precision.HIGHEST, preferred_element_type=F32
        )

    half = out_ref.shape[1]
    own, other = left_half(own_ref), left_half(other_ref)
    is_first = core_ref[0] == 0
    p = jnp.concatenate([jnp.where(is_first, own, other), jnp.where(is_first, other, own)], axis=0)
    p = p * lax.rsqrt(jnp.sum(p * p, axis=0, keepdims=True))
    inverse = inverse_factor(product(p, p, ((0,), (0,))))
    basis = product(p, inverse, ((1,), (1,))).astype(BF16)
    out_ref[0] = basis[:half, :]
    out_ref[1] = basis[half:, :]


def bases(core, own, other, half):
    vmem = pl.BlockSpec(memory_space=pltpu.VMEM)
    return pl.pallas_call(
        basis_kernel,
        out_shape=jax.ShapeDtypeStruct((2, half, LANES), BF16),
        in_specs=[pl.BlockSpec(memory_space=pltpu.SMEM), vmem, vmem],
        out_specs=vmem,
        compiler_params=params(),
        name="basis",
    )(core, own, other)


def finish_kernel(
    replicas,
    core_ref,
    own_ref,
    other_ref,
    own_sum_ref,
    other_sum_ref,
    basis_ref,
    error_out,
    q_out,
    error_ref,
    q_ref,
    sems,
):
    core = core_ref[0]
    half = basis_ref.shape[1]

    def slab_of(ref, slab):
        at, end, parts = slab * half, (slab + 1) * half, []
        while at < min(end, CHIPS * MAIN):
            piece = at // MAIN
            stop = min(end, (piece + 1) * MAIN)
            parts.append(ref[piece, at - piece * MAIN : stop - piece * MAIN, :])
            at = stop
        if at < end:
            extra = [ref[piece, MAIN : MAIN + 16, :].astype(F32)[:8, :] for piece in range(CHIPS)]
            parts.append(jnp.concatenate(extra, axis=0).astype(BF16))
        return jnp.concatenate(parts, axis=0)

    def pair_of(read, pair):
        return jnp.concatenate([read(2 * pair), read(2 * pair + 1)], axis=1)

    basis = (basis_ref[core], basis_ref[1 - core])
    flipped = [b.astype(F32).T.astype(BF16) for b in basis]
    copies = []
    pairs = q_ref.shape[0] // (2 * LANES)

    def right_of(pair):
        terms = [
            jnp.dot(flat, pair_of(lambda slab: slab_of(ref, slab), pair), preferred_element_type=F32)
            for flat, ref in zip(flipped, (own_sum_ref, other_sum_ref))
        ]
        return (terms[0] + terms[1]) * (1.0 / replicas)

    def send(source, target, sem):
        copies.append(pltpu.make_async_copy(source, target, sem))
        copies[-1].start()

    ready = [right_of(pair) for pair in range(2)]
    for pair in range(pairs):
        columns = slice(2 * pair * LANES, 2 * (pair + 1) * LANES)
        scaled = ready.pop(0)
        right = scaled.astype(BF16)
        if pair + 2 < pairs:
            ready.append(right_of(pair + 2))
        products = [jnp.dot(b, right, preferred_element_type=F32) for b in basis]
        for at, (which, ref) in enumerate(((core, own_ref), (1 - core, other_ref))):
            mine = pair_of(lambda slab: ref[slab * half : (slab + 1) * half, :], pair).astype(F32)
            rows = pl.ds(pl.multiple_of(which * half, half), half)
            error_ref[rows, columns] = (mine - products[at]).astype(BF16)
            send(error_ref.at[rows, columns], error_out.at[rows, columns], sems.at[at, pair])
        q_ref[columns, :] = scaled.T.astype(BF16)
        send(q_ref.at[columns, :], q_out.at[columns, :], sems.at[2, pair])
    for copy in copies:
        copy.wait()


def finish(core, own, other, own_sum, other_sum, basis, replicas):
    rows, cols = 2 * basis.shape[1], own.shape[0] // basis.shape[1] * LANES
    vmem = pl.BlockSpec(memory_space=pltpu.VMEM)
    return pl.pallas_call(
        lambda *refs: finish_kernel(replicas, *refs),
        out_shape=(jax.ShapeDtypeStruct((rows, cols), BF16), jax.ShapeDtypeStruct((cols, LANES), BF16)),
        in_specs=[pl.BlockSpec(memory_space=pltpu.SMEM)] + [vmem] * 5,
        out_specs=(pl.BlockSpec(memory_space=pl.ANY),) * 2,
        scratch_shapes=[
            pltpu.VMEM((rows, cols), BF16),
            pltpu.VMEM((cols, LANES), BF16),
            pltpu.SemaphoreType.DMA((3, cols // (2 * LANES))),
        ],
        compiler_params=params(),
        name="finish",
    )(core, own, other, own_sum, other_sum, basis)


def on_device(gradient, error, q_prev):
    rows, cols = gradient.shape[1:]
    replicas = lax.axis_size("dp")
    half = rows // 2
    core = (lax.axis_index("dp") % 2).astype(jnp.int32).reshape(1)
    twin = [(i, i ^ 1) for i in range(replicas)]
    same_core = [[2 * chip + c for chip in range(CHIPS)] for c in range(2)]

    def across_chips(pieces):
        return lax.all_to_all(pieces, "dp", 0, 0, axis_index_groups=same_core)

    other = half_call(sent_kernel, SENT_LIMIT, core, gradient[0], error[0])
    got = lax.ppermute(other, "dp", twin)
    own, p_own = half_call(kept_kernel, KEPT_LIMIT, core, gradient[0], error[0], q_prev)
    pieces = across_chips(pack(own, got, p_own, q_prev))
    left, total = sums(pieces, lax.axis_size("tensor"))
    left = lax.all_to_all(left, "tensor", 0, 0)
    gathered = across_chips(repack(left, total))
    gathered_other = lax.ppermute(gathered, "dp", twin)
    basis = bases(core, gathered, gathered_other, half)
    new_error, q_next = finish(core, own, other, gathered, gathered_other, basis, replicas)
    return (new_error[None], q_next)


def solution(mesh):
    placed = (P("dp", None, "tensor"), P("dp", None, "tensor"), P("tensor", None))
    return jax.shard_map(
        on_device,
        mesh=mesh,
        in_specs=placed,
        out_specs=(P("dp", None, "tensor"), P("tensor", None)),
        check_vma=False,
    )
```

```python
import jax
import jax.numpy as jnp
from jax import lax
from jax.experimental import pallas as pl
from jax.experimental.pallas import tpu as pltpu
from jax.sharding import PartitionSpec as P

F32, BF16 = jnp.float32, jnp.bfloat16
LANES = 128
CHIPS = 16
MAIN = 160
MIXED = 32
VMEM_LIMIT = 48 * 1024 * 1024
SENT_LIMIT = 52 * 1024 * 1024
KEPT_LIMIT = 52 * 1024 * 1024


def params():
    return pltpu.CompilerParams(vmem_limit_bytes=VMEM_LIMIT)


def combined_half(which, g_in, e_in, out_ref, g_ref, e_ref, sems):
    half, cols = g_ref.shape
    chunks = sems.shape[1]
    count = half // chunks
    copies = []
    for chunk in range(chunks):
        rows = pl.ds(pl.multiple_of(which * half + chunk * count, 16), count)
        here = slice(chunk * count, (chunk + 1) * count)
        pair = [
            pltpu.make_async_copy(g_in.at[rows, :], g_ref.at[here, :], sems.at[0, chunk]),
            pltpu.make_async_copy(e_in.at[rows, :], e_ref.at[here, :], sems.at[1, chunk]),
        ]
        for copy in pair:
            copy.start()
        copies.append(pair)
    for chunk in range(chunks):
        for copy in copies[chunk]:
            copy.wait()
        here = slice(chunk * count, (chunk + 1) * count)
        total = (g_ref[here, :].astype(F32) + e_ref[here, :].astype(F32)).astype(BF16)
        for slab in range(cols // LANES):
            first = slab * half + chunk * count
            out_ref[first : first + count, :] = total[:, slab * LANES : (slab + 1) * LANES]


def sent_kernel(core_ref, g_in, e_in, out_ref, *scratch):
    combined_half(1 - core_ref[0], g_in, e_in, out_ref, *scratch)


def kept_kernel(core_ref, g_in, e_in, q_ref, out_ref, p_ref, *scratch):
    combined_half(core_ref[0], g_in, e_in, out_ref, *scratch)
    p_ref[...] = slab_product(out_ref, q_ref, p_ref.shape[0])


def slab_product(slabs_ref, q_ref, half):
    p = jnp.zeros((half, LANES), F32)
    for pair in range(q_ref.shape[0] // (2 * LANES)):
        two = [slabs_ref[(2 * pair + k) * half : (2 * pair + k + 1) * half, :] for k in range(2)]
        q = q_ref[2 * pair * LANES : 2 * (pair + 1) * LANES, :]
        p += jnp.dot(jnp.concatenate(two, axis=1), q, preferred_element_type=F32)
    return p


def half_call(kernel, limit, core, gradient, error, *more):
    rows, cols = gradient.shape
    half = rows // 2
    chunks = 2
    out = jax.ShapeDtypeStruct((cols // LANES * half, LANES), BF16)
    vmem = pl.BlockSpec(memory_space=pltpu.VMEM)
    anywhere = pl.BlockSpec(memory_space=pl.ANY)
    return pl.pallas_call(
        kernel,
        out_shape=(out, jax.ShapeDtypeStruct((half, LANES), F32)) if more else out,
        in_specs=[pl.BlockSpec(memory_space=pltpu.SMEM), anywhere, anywhere] + [vmem] * len(more),
        out_specs=(vmem, vmem) if more else vmem,
        scratch_shapes=[
            pltpu.VMEM((half, cols), BF16),
            pltpu.VMEM((half, cols), BF16),
            pltpu.SemaphoreType.DMA((2, chunks)),
        ],
        compiler_params=pltpu.CompilerParams(vmem_limit_bytes=limit),
        name="kept" if more else "sent",
    )(core, gradient, error, *more)


def upper_rows():
    return lax.broadcasted_iota(jnp.int32, (8, LANES), 0) < 4


def swap(x):
    return jnp.concatenate([x[4:, :], x[:4, :]], axis=0)


def high_low(x):
    high = x.astype(BF16).astype(F32)
    return high, x - high


def joined(eight, four):
    high, low = high_low(eight)
    high4, low4 = high_low(four)
    return jnp.concatenate([high, low, jnp.where(upper_rows(), high4, low4)], axis=0)


def parted(x):
    return x[:8, :] + x[8:16, :], x[16:, :] + swap(x[16:, :])


def pack_kernel(own_ref, got_ref, p_ref, q_ref, out_ref):
    half = p_ref.shape[0]
    p = p_ref[...] + slab_product(got_ref, q_ref, half)
    for piece in range(CHIPS):
        rows = slice(piece * MAIN, (piece + 1) * MAIN)
        out_ref[piece, :MAIN, :] = (own_ref[rows, :].astype(F32) + got_ref[rows, :].astype(F32)).astype(BF16)
    last = slice(CHIPS * MAIN, CHIPS * (MAIN + 8))
    extra = own_ref[last, :].astype(F32) + got_ref[last, :].astype(F32)
    for piece in range(CHIPS):
        both = p[8 * (CHIPS + piece // 2) : 8 * (CHIPS + piece // 2 + 1), :]
        four = jnp.where(upper_rows() == (piece % 2 == 0), both, swap(both))
        mixed = [extra[8 * piece : 8 * piece + 8, :], joined(p[8 * piece : 8 * piece + 8, :], four)]
        out_ref[piece, MAIN:, :] = jnp.concatenate(mixed, axis=0).astype(BF16)


def pack(own, got, p_own, q_prev):
    return pl.pallas_call(
        pack_kernel,
        out_shape=jax.ShapeDtypeStruct((CHIPS, MAIN + MIXED, LANES), BF16),
        compiler_params=params(),
        name="pack",
    )(own, got, p_own, q_prev)


def sums_kernel(in_ref, left_ref, total_ref):
    total = in_ref[0].astype(F32)
    for chip in range(1, CHIPS):
        total += in_ref[chip].astype(F32)
    left = joined(*parted(total[MAIN + 8 :, :])).astype(BF16)
    for copy in range(left_ref.shape[0]):
        left_ref[copy] = left
    total_ref[...] = total[: MAIN + 8, :]


def sums(pieces, copies):
    return pl.pallas_call(
        sums_kernel,
        out_shape=(
            jax.ShapeDtypeStruct((copies, MIXED - 8, LANES), BF16),
            jax.ShapeDtypeStruct((MAIN + 8, LANES), F32),
        ),
        compiler_params=params(),
        name="sums",
    )(pieces)


def repack_kernel(left_ref, total_ref, out_ref):
    left = left_ref[0].astype(F32)
    for at in range(1, left_ref.shape[0]):
        left += left_ref[at].astype(F32)
    piece = jnp.concatenate([total_ref[...], joined(*parted(left))], axis=0).astype(BF16)
    for chip in range(CHIPS):
        out_ref[chip] = piece


def repack(left, total):
    return pl.pallas_call(
        repack_kernel,
        out_shape=jax.ShapeDtypeStruct((CHIPS, MAIN + MIXED, LANES), BF16),
        compiler_params=params(),
        name="repack",
    )(left, total)


def spread(x, row=None, lane=None):
    if row is not None:
        x = x[row : row + 1, :]
    if lane is not None:
        x = x[:, lane : lane + 1]
    return jnp.broadcast_to(x, (8, LANES))


def added(terms):
    while len(terms) > 1:
        terms = [terms[i] + terms[i + 1] for i in range(0, len(terms), 2)]
    return terms[0]


def inverse_factor(gram):
    width = 8
    groups = LANES // width
    w = [gram[width * g : width * (g + 1), :] for g in range(groups)]
    row_of = lax.broadcasted_iota(jnp.int32, (width, LANES), 0)
    lane_of = lax.broadcasted_iota(jnp.int32, (width, LANES), 1)
    pivots = [spread(w[0], lane=i) for i in range(width)]
    for g in range(groups):
        first = width * g
        more = g + 1 < groups
        column = {h: [spread(w[h], lane=first + i) for i in range(width)] for h in range(g + 1, groups)}
        ahead = [spread(w[g + 1], lane=first + width + n) for n in range(width)] if more else []
        inside = (lane_of >= first) & (lane_of < first + width)
        start = jnp.where(inside, jnp.where(lane_of - first == row_of, 1.0, 0.0), w[g])
        y = [spread(start, row=m) for m in range(width)]
        d = [[spread(pivots[i], row=m) for i in range(m + 1)] for m in range(width)]
        low = [[None] * width for _ in range(width)]
        root = [None] * width
        lead = list(column[g + 1]) if more else None
        for i in range(width):
            if i % 2 == 0:
                first_root = lax.rsqrt(d[i][i])
                det = d[i][i] * d[i + 1][i + 1] - d[i + 1][i] * d[i + 1][i]
                root[i] = first_root
                root[i + 1] = d[i][i] * first_root * lax.rsqrt(det)
            for m in range(i + 1, width):
                low[m][i] = d[m][i] * root[i]
            for m in range(i + 1, width):
                for n in range(i + 1, m + 1):
                    if i % 2 == 1 or m > i + 1:
                        d[m][n] = d[m][n] - low[m][i] * low[n][i]
            y[i] = y[i] * root[i]
            for m in range(i + 1, width):
                y[m] = y[m] - low[m][i] * y[i]
            if more:
                lead[i] = lead[i] * root[i]
                for m in range(i + 1, width):
                    lead[m] = lead[m] - low[m][i] * lead[i]
        z = [None] * width
        for m in reversed(range(width)):
            value = y[m]
            for k in range(m + 1, width):
                value = value - low[k][m] * z[k]
            z[m] = value * root[m]
        for h in range(g + 1, groups):
            left, right = (lead, y) if h == g + 1 else (column[h], z)
            w[h] = jnp.where(inside, 0.0, w[h]) - added([left[i] * right[i] for i in range(width)])
        pivots = [
            ahead[n] - added([lead[i] * spread(lead[i], row=n) for i in range(width)]) for n in range(len(ahead))
        ]
        rows = y[0]
        for m in range(1, width):
            rows = jnp.where(row_of == m, y[m], rows)
        w[g] = jnp.where(lane_of <= row_of + first, rows, 0.0)
    return jnp.concatenate(w, axis=0)


def left_half(ref):
    parts = [parted(ref[piece, MAIN:, :].astype(F32)[8:, :]) for piece in range(CHIPS)]
    lower = [jnp.where(upper_rows(), parts[2 * k][1], parts[2 * k + 1][1]) for k in range(CHIPS // 2)]
    return jnp.concatenate([eight for eight, _ in parts] + lower, axis=0)


def own_rows_kernel(in_ref, out_ref):
    out_ref[...] = left_half(in_ref)


def own_rows(pieces, half):
    return pl.pallas_call(
        own_rows_kernel,
        out_shape=jax.ShapeDtypeStruct((half, LANES), F32),
        compiler_params=params(),
        name="own_rows",
    )(pieces)


def flipped_basis(p):
    def product(x, y):
        return jnp.dot(x, y, precision=lax.Precision.HIGHEST, preferred_element_type=F32)

    p = p * lax.rsqrt(jnp.sum(p * p, axis=0, keepdims=True))
    flipped = p.T
    return product(inverse_factor(product(flipped, p)), flipped)


def finish_kernel(
    replicas,
    core_ref,
    own_ref,
    other_ref,
    own_sum_ref,
    other_sum_ref,
    p_ref,
    error_out,
    q_out,
    error_ref,
    q_ref,
    basis_ref,
    sems,
):
    core = core_ref[0]
    half = p_ref.shape[0]

    def slab_of(ref, slab):
        at, end, parts = slab * half, (slab + 1) * half, []
        while at < min(end, CHIPS * MAIN):
            piece = at // MAIN
            stop = min(end, (piece + 1) * MAIN)
            parts.append(ref[piece, at - piece * MAIN : stop - piece * MAIN, :])
            at = stop
        if at < end:
            extra = [ref[piece, MAIN : MAIN + 16, :].astype(F32)[:8, :] for piece in range(CHIPS)]
            parts.append(jnp.concatenate(extra, axis=0).astype(BF16))
        return jnp.concatenate(parts, axis=0)

    def pair_of(read, pair):
        return jnp.concatenate([read(2 * pair), read(2 * pair + 1)], axis=1)

    is_first = core == 0

    def in_order(own, other):
        return jnp.concatenate([jnp.where(is_first, own, other), jnp.where(is_first, other, own)], axis=0)

    flipped = flipped_basis(in_order(p_ref[...], left_half(other_sum_ref)))
    rows_of_basis = flipped.T.astype(BF16)
    flipped = flipped.astype(BF16)
    basis_ref[0] = rows_of_basis[:half, :]
    basis_ref[1] = rows_of_basis[half:, :]
    basis = (basis_ref[core], basis_ref[1 - core])
    copies = []
    pairs = q_ref.shape[0] // (2 * LANES)

    def right_of(pair):
        sums = in_order(*(pair_of(lambda slab: slab_of(ref, slab), pair) for ref in (own_sum_ref, other_sum_ref)))
        return jnp.dot(flipped, sums, preferred_element_type=F32) * (1.0 / replicas)

    def send(source, target, sem):
        copies.append(pltpu.make_async_copy(source, target, sem))
        copies[-1].start()

    ready = [right_of(pair) for pair in range(2)]
    for pair in range(pairs):
        columns = slice(2 * pair * LANES, 2 * (pair + 1) * LANES)
        scaled = ready.pop(0)
        right = scaled.astype(BF16)
        if pair + 2 < pairs:
            ready.append(right_of(pair + 2))
        products = [jnp.dot(b, right, preferred_element_type=F32) for b in basis]
        for at, (which, ref) in enumerate(((core, own_ref), (1 - core, other_ref))):
            mine = pair_of(lambda slab: ref[slab * half : (slab + 1) * half, :], pair).astype(F32)
            rows = pl.ds(pl.multiple_of(which * half, half), half)
            error_ref[rows, columns] = (mine - products[at]).astype(BF16)
            send(error_ref.at[rows, columns], error_out.at[rows, columns], sems.at[at, pair])
        q_ref[columns, :] = scaled.T.astype(BF16)
        send(q_ref.at[columns, :], q_out.at[columns, :], sems.at[2, pair])
    for copy in copies:
        copy.wait()


def finish(core, own, other, own_sum, other_sum, p_own, cols, replicas):
    rows = 2 * p_own.shape[0]
    vmem = pl.BlockSpec(memory_space=pltpu.VMEM)
    return pl.pallas_call(
        lambda *refs: finish_kernel(replicas, *refs),
        out_shape=(jax.ShapeDtypeStruct((rows, cols), BF16), jax.ShapeDtypeStruct((cols, LANES), BF16)),
        in_specs=[pl.BlockSpec(memory_space=pltpu.SMEM)] + [vmem] * 5,
        out_specs=(pl.BlockSpec(memory_space=pl.ANY),) * 2,
        scratch_shapes=[
            pltpu.VMEM((rows, cols), BF16),
            pltpu.VMEM((cols, LANES), BF16),
            pltpu.VMEM((2, rows // 2, LANES), BF16),
            pltpu.SemaphoreType.DMA((3, cols // (2 * LANES))),
        ],
        compiler_params=params(),
        name="finish",
    )(core, own, other, own_sum, other_sum, p_own)


def on_device(gradient, error, q_prev):
    rows, cols = gradient.shape[1:]
    replicas = lax.axis_size("dp")
    half = rows // 2
    core = (lax.axis_index("dp") % 2).astype(jnp.int32).reshape(1)
    twin = [(i, i ^ 1) for i in range(replicas)]
    same_core = [[2 * chip + c for chip in range(CHIPS)] for c in range(2)]

    def across_chips(pieces):
        return lax.all_to_all(pieces, "dp", 0, 0, axis_index_groups=same_core)

    other = half_call(sent_kernel, SENT_LIMIT, core, gradient[0], error[0])
    got = lax.ppermute(other, "dp", twin)
    own, p_own = half_call(kept_kernel, KEPT_LIMIT, core, gradient[0], error[0], q_prev)
    pieces = across_chips(pack(own, got, p_own, q_prev))
    left, total = sums(pieces, lax.axis_size("tensor"))
    left = lax.all_to_all(left, "tensor", 0, 0)
    gathered = across_chips(repack(left, total))
    gathered_other = lax.ppermute(gathered, "dp", twin)
    p_own = own_rows(gathered, half)
    new_error, q_next = finish(core, own, other, gathered, gathered_other, p_own, cols, replicas)
    return (new_error[None], q_next)


def solution(mesh):
    placed = (P("dp", None, "tensor"), P("dp", None, "tensor"), P("tensor", None))
    return jax.shard_map(
        on_device,
        mesh=mesh,
        in_specs=placed,
        out_specs=(P("dp", None, "tensor"), P("tensor", None)),
        check_vma=False,
    )
```

```python
import jax
import jax.numpy as jnp
from jax import lax
from jax.experimental import pallas as pl
from jax.experimental.pallas import tpu as pltpu
from jax.sharding import PartitionSpec as P

F32, BF16 = jnp.float32, jnp.bfloat16
LANES = 128
CHIPS = 16
MAIN = 160
MIXED = 32
ORDERS = (
    [10, 11, 8, 13, 14, 0, 9, 7, 6, 15, 1, 3, 2, 12, 4, 5],
    [5, 6, 10, 11, 8, 4, 7, 0, 1, 15, 2, 3, 13, 14, 9, 12],
)
VMEM_LIMIT = 48 * 1024 * 1024
SENT_LIMIT = 52 * 1024 * 1024
KEPT_LIMIT = 52 * 1024 * 1024


def params():
    return pltpu.CompilerParams(vmem_limit_bytes=VMEM_LIMIT)


def combined_half(which, g_in, e_in, out_ref, g_ref, e_ref, sems):
    half, cols = g_ref.shape
    chunks = sems.shape[1]
    count = half // chunks
    copies = []
    for chunk in range(chunks):
        rows = pl.ds(pl.multiple_of(which * half + chunk * count, 16), count)
        here = slice(chunk * count, (chunk + 1) * count)
        pair = [
            pltpu.make_async_copy(g_in.at[rows, :], g_ref.at[here, :], sems.at[0, chunk]),
            pltpu.make_async_copy(e_in.at[rows, :], e_ref.at[here, :], sems.at[1, chunk]),
        ]
        for copy in pair:
            copy.start()
        copies.append(pair)
    for chunk in range(chunks):
        for copy in copies[chunk]:
            copy.wait()
        here = slice(chunk * count, (chunk + 1) * count)
        total = (g_ref[here, :].astype(F32) + e_ref[here, :].astype(F32)).astype(BF16)
        for slab in range(cols // LANES):
            first = slab * half + chunk * count
            out_ref[first : first + count, :] = total[:, slab * LANES : (slab + 1) * LANES]


def sent_kernel(core_ref, g_in, e_in, out_ref, *scratch):
    combined_half(1 - core_ref[0], g_in, e_in, out_ref, *scratch)


def kept_kernel(core_ref, g_in, e_in, q_ref, out_ref, p_ref, *scratch):
    combined_half(core_ref[0], g_in, e_in, out_ref, *scratch)
    p_ref[...] = slab_product(out_ref, q_ref, p_ref.shape[0])


def slab_product(slabs_ref, q_ref, half):
    p = jnp.zeros((half, LANES), F32)
    for pair in range(q_ref.shape[0] // (2 * LANES)):
        two = [slabs_ref[(2 * pair + k) * half : (2 * pair + k + 1) * half, :] for k in range(2)]
        q = q_ref[2 * pair * LANES : 2 * (pair + 1) * LANES, :]
        p += jnp.dot(jnp.concatenate(two, axis=1), q, preferred_element_type=F32)
    return p


def half_call(kernel, limit, core, gradient, error, *more):
    rows, cols = gradient.shape
    half = rows // 2
    chunks = 2
    out = jax.ShapeDtypeStruct((cols // LANES * half, LANES), BF16)
    vmem = pl.BlockSpec(memory_space=pltpu.VMEM)
    anywhere = pl.BlockSpec(memory_space=pl.ANY)
    return pl.pallas_call(
        kernel,
        out_shape=(out, jax.ShapeDtypeStruct((half, LANES), F32)) if more else out,
        in_specs=[pl.BlockSpec(memory_space=pltpu.SMEM), anywhere, anywhere] + [vmem] * len(more),
        out_specs=(vmem, vmem) if more else vmem,
        scratch_shapes=[
            pltpu.VMEM((half, cols), BF16),
            pltpu.VMEM((half, cols), BF16),
            pltpu.SemaphoreType.DMA((2, chunks)),
        ],
        compiler_params=pltpu.CompilerParams(vmem_limit_bytes=limit),
        name="kept" if more else "sent",
    )(core, gradient, error, *more)


def upper_rows():
    return lax.broadcasted_iota(jnp.int32, (8, LANES), 0) < 4


def swap(x):
    return jnp.concatenate([x[4:, :], x[:4, :]], axis=0)


def high_low(x):
    high = x.astype(BF16).astype(F32)
    return high, x - high


def joined(eight, four):
    high, low = high_low(eight)
    high4, low4 = high_low(four)
    return jnp.concatenate([high, low, jnp.where(upper_rows(), high4, low4)], axis=0)


def parted(x):
    return x[:8, :] + x[8:16, :], x[16:, :] + swap(x[16:, :])


def pack_kernel(own_ref, got_ref, p_ref, q_ref, out_ref):
    half = p_ref.shape[0]
    p = p_ref[...] + slab_product(got_ref, q_ref, half)
    for piece in range(CHIPS):
        rows = slice(piece * MAIN, (piece + 1) * MAIN)
        out_ref[piece, :MAIN, :] = (own_ref[rows, :].astype(F32) + got_ref[rows, :].astype(F32)).astype(BF16)
    last = slice(CHIPS * MAIN, CHIPS * (MAIN + 8))
    extra = own_ref[last, :].astype(F32) + got_ref[last, :].astype(F32)
    for piece in range(CHIPS):
        both = p[8 * (CHIPS + piece // 2) : 8 * (CHIPS + piece // 2 + 1), :]
        four = jnp.where(upper_rows() == (piece % 2 == 0), both, swap(both))
        mixed = [extra[8 * piece : 8 * piece + 8, :], joined(p[8 * piece : 8 * piece + 8, :], four)]
        out_ref[piece, MAIN:, :] = jnp.concatenate(mixed, axis=0).astype(BF16)


def pack(own, got, p_own, q_prev):
    return pl.pallas_call(
        pack_kernel,
        out_shape=jax.ShapeDtypeStruct((CHIPS, MAIN + MIXED, LANES), BF16),
        compiler_params=params(),
        name="pack",
    )(own, got, p_own, q_prev)


def sums_kernel(in_ref, left_ref, total_ref):
    total = in_ref[0].astype(F32)
    for chip in range(1, CHIPS):
        total += in_ref[chip].astype(F32)
    left = joined(*parted(total[MAIN + 8 :, :])).astype(BF16)
    for copy in range(left_ref.shape[0]):
        left_ref[copy] = left
    total_ref[...] = total[: MAIN + 8, :]


def sums(pieces, copies):
    return pl.pallas_call(
        sums_kernel,
        out_shape=(
            jax.ShapeDtypeStruct((copies, MIXED - 8, LANES), BF16),
            jax.ShapeDtypeStruct((MAIN + 8, LANES), F32),
        ),
        compiler_params=params(),
        name="sums",
    )(pieces)


def repack_kernel(left_ref, total_ref, out_ref):
    left = left_ref[0].astype(F32)
    for at in range(1, left_ref.shape[0]):
        left += left_ref[at].astype(F32)
    piece = jnp.concatenate([total_ref[...], joined(*parted(left))], axis=0).astype(BF16)
    for chip in range(CHIPS):
        out_ref[chip] = piece


def repack(left, total):
    return pl.pallas_call(
        repack_kernel,
        out_shape=jax.ShapeDtypeStruct((CHIPS, MAIN + MIXED, LANES), BF16),
        compiler_params=params(),
        name="repack",
    )(left, total)


def spread(x, row=None, lane=None):
    if row is not None:
        x = x[row : row + 1, :]
    if lane is not None:
        x = x[:, lane : lane + 1]
    return jnp.broadcast_to(x, (8, LANES))


def added(terms):
    while len(terms) > 1:
        terms = [terms[i] + terms[i + 1] for i in range(0, len(terms), 2)]
    return terms[0]


def inverse_factor(gram):
    width = 8
    groups = LANES // width
    w = [gram[width * g : width * (g + 1), :] for g in range(groups)]
    row_of = lax.broadcasted_iota(jnp.int32, (width, LANES), 0)
    lane_of = lax.broadcasted_iota(jnp.int32, (width, LANES), 1)
    pivots = [spread(w[0], lane=i) for i in range(width)]
    for g in range(groups):
        first = width * g
        more = g + 1 < groups
        column = {h: [spread(w[h], lane=first + i) for i in range(width)] for h in range(g + 1, groups)}
        ahead = [spread(w[g + 1], lane=first + width + n) for n in range(width)] if more else []
        inside = (lane_of >= first) & (lane_of < first + width)
        start = jnp.where(inside, jnp.where(lane_of - first == row_of, 1.0, 0.0), w[g])
        y = [spread(start, row=m) for m in range(width)]
        d = [[spread(pivots[i], row=m) for i in range(m + 1)] for m in range(width)]
        low = [[None] * width for _ in range(width)]
        root = [None] * width
        lead = list(column[g + 1]) if more else None
        for i in range(width):
            if i % 2 == 0:
                first_root = lax.rsqrt(d[i][i])
                det = d[i][i] * d[i + 1][i + 1] - d[i + 1][i] * d[i + 1][i]
                root[i] = first_root
                root[i + 1] = d[i][i] * first_root * lax.rsqrt(det)
            for m in range(i + 1, width):
                low[m][i] = d[m][i] * root[i]
            for m in range(i + 1, width):
                for n in range(i + 1, m + 1):
                    if i % 2 == 1 or m > i + 1:
                        d[m][n] = d[m][n] - low[m][i] * low[n][i]
            y[i] = y[i] * root[i]
            for m in range(i + 1, width):
                y[m] = y[m] - low[m][i] * y[i]
            if more:
                lead[i] = lead[i] * root[i]
                for m in range(i + 1, width):
                    lead[m] = lead[m] - low[m][i] * lead[i]
        z = [None] * width
        for m in reversed(range(width)):
            value = y[m]
            for k in range(m + 1, width):
                value = value - low[k][m] * z[k]
            z[m] = value * root[m]
        for h in range(g + 1, groups):
            left, right = (lead, y) if h == g + 1 else (column[h], z)
            w[h] = jnp.where(inside, 0.0, w[h]) - added([left[i] * right[i] for i in range(width)])
        pivots = [
            ahead[n] - added([lead[i] * spread(lead[i], row=n) for i in range(width)]) for n in range(len(ahead))
        ]
        rows = y[0]
        for m in range(1, width):
            rows = jnp.where(row_of == m, y[m], rows)
        w[g] = jnp.where(lane_of <= row_of + first, rows, 0.0)
    return jnp.concatenate(w, axis=0)


def basis_kernel(core_ref, own_ref, other_ref, out_ref):
    def left_half(ref):
        parts = [parted(ref[piece, MAIN:, :].astype(F32)[8:, :]) for piece in range(CHIPS)]
        lower = [jnp.where(upper_rows(), parts[2 * k][1], parts[2 * k + 1][1]) for k in range(CHIPS // 2)]
        return jnp.concatenate([eight for eight, _ in parts] + lower, axis=0)

    def product(x, y, dims):
        return lax.dot_general(
            x, y, (dims, ((), ())), precision=lax.Precision.HIGHEST, preferred_element_type=F32
        )

    half = out_ref.shape[1]
    own, other = left_half(own_ref), left_half(other_ref)
    is_first = core_ref[0] == 0
    p = jnp.concatenate([jnp.where(is_first, own, other), jnp.where(is_first, other, own)], axis=0)
    p = p * lax.rsqrt(jnp.sum(p * p, axis=0, keepdims=True))
    inverse = inverse_factor(product(p, p, ((0,), (0,))))
    basis = product(p, inverse, ((1,), (1,))).astype(BF16)
    out_ref[0] = basis[:half, :]
    out_ref[1] = basis[half:, :]


def bases(core, own, other, half):
    vmem = pl.BlockSpec(memory_space=pltpu.VMEM)
    return pl.pallas_call(
        basis_kernel,
        out_shape=jax.ShapeDtypeStruct((2, half, LANES), BF16),
        in_specs=[pl.BlockSpec(memory_space=pltpu.SMEM), vmem, vmem],
        out_specs=vmem,
        compiler_params=params(),
        name="basis",
    )(core, own, other)


def finish_kernel(
    replicas,
    core_ref,
    own_ref,
    other_ref,
    own_sum_ref,
    other_sum_ref,
    basis_ref,
    error_out,
    q_out,
    error_ref,
    q_ref,
    sems,
):
    core = core_ref[0]
    half = basis_ref.shape[1]

    def slab_of(ref, slab):
        at, end, parts = slab * half, (slab + 1) * half, []
        while at < min(end, CHIPS * MAIN):
            piece = at // MAIN
            stop = min(end, (piece + 1) * MAIN)
            parts.append(ref[piece, at - piece * MAIN : stop - piece * MAIN, :])
            at = stop
        if at < end:
            extra = [ref[piece, MAIN : MAIN + 16, :].astype(F32)[:8, :] for piece in range(CHIPS)]
            parts.append(jnp.concatenate(extra, axis=0).astype(BF16))
        return jnp.concatenate(parts, axis=0)

    def pair_of(read, pair):
        return jnp.concatenate([read(2 * pair), read(2 * pair + 1)], axis=1)

    basis = (basis_ref[core], basis_ref[1 - core])
    flipped = [b.astype(F32).T.astype(BF16) for b in basis]
    copies = []
    pairs = q_ref.shape[0] // (2 * LANES)

    def right_of(pair):
        terms = [
            jnp.dot(flat, pair_of(lambda slab: slab_of(ref, slab), pair), preferred_element_type=F32)
            for flat, ref in zip(flipped, (own_sum_ref, other_sum_ref))
        ]
        return (terms[0] + terms[1]) * (1.0 / replicas)

    def send(source, target, sem):
        copies.append(pltpu.make_async_copy(source, target, sem))
        copies[-1].start()

    ready = [right_of(pair) for pair in range(2)]
    for pair in range(pairs):
        columns = slice(2 * pair * LANES, 2 * (pair + 1) * LANES)
        scaled = ready.pop(0)
        right = scaled.astype(BF16)
        if pair + 2 < pairs:
            ready.append(right_of(pair + 2))
        products = [jnp.dot(b, right, preferred_element_type=F32) for b in basis]
        for at, (which, ref) in enumerate(((core, own_ref), (1 - core, other_ref))):
            mine = pair_of(lambda slab: ref[slab * half : (slab + 1) * half, :], pair).astype(F32)
            rows = pl.ds(pl.multiple_of(which * half, half), half)
            error_ref[rows, columns] = (mine - products[at]).astype(BF16)
            send(error_ref.at[rows, columns], error_out.at[rows, columns], sems.at[at, pair])
        q_ref[columns, :] = scaled.T.astype(BF16)
        send(q_ref.at[columns, :], q_out.at[columns, :], sems.at[2, pair])
    for copy in copies:
        copy.wait()


def finish(core, own, other, own_sum, other_sum, basis, replicas):
    rows, cols = 2 * basis.shape[1], own.shape[0] // basis.shape[1] * LANES
    vmem = pl.BlockSpec(memory_space=pltpu.VMEM)
    return pl.pallas_call(
        lambda *refs: finish_kernel(replicas, *refs),
        out_shape=(jax.ShapeDtypeStruct((rows, cols), BF16), jax.ShapeDtypeStruct((cols, LANES), BF16)),
        in_specs=[pl.BlockSpec(memory_space=pltpu.SMEM)] + [vmem] * 5,
        out_specs=(pl.BlockSpec(memory_space=pl.ANY),) * 2,
        scratch_shapes=[
            pltpu.VMEM((rows, cols), BF16),
            pltpu.VMEM((cols, LANES), BF16),
            pltpu.SemaphoreType.DMA((3, cols // (2 * LANES))),
        ],
        compiler_params=params(),
        name="finish",
    )(core, own, other, own_sum, other_sum, basis)


def on_device(gradient, error, q_prev):
    rows, cols = gradient.shape[1:]
    replicas = lax.axis_size("dp")
    half = rows // 2
    core = (lax.axis_index("dp") % 2).astype(jnp.int32).reshape(1)
    twin = [(i, i ^ 1) for i in range(replicas)]
    same_core = [[2 * chip + c for chip in ORDERS[c]] for c in range(2)]

    def across_chips(pieces):
        return lax.all_to_all(pieces, "dp", 0, 0, axis_index_groups=same_core)

    other = half_call(sent_kernel, SENT_LIMIT, core, gradient[0], error[0])
    got = lax.ppermute(other, "dp", twin)
    own, p_own = half_call(kept_kernel, KEPT_LIMIT, core, gradient[0], error[0], q_prev)
    pieces = across_chips(pack(own, got, p_own, q_prev))
    left, total = sums(pieces, lax.axis_size("tensor"))
    left = lax.all_to_all(left, "tensor", 0, 0)
    gathered = across_chips(repack(left, total))
    gathered_other = lax.ppermute(gathered, "dp", twin)
    basis = bases(core, gathered, gathered_other, half)
    new_error, q_next = finish(core, own, other, gathered, gathered_other, basis, replicas)
    return (new_error[None], q_next)


def solution(mesh):
    placed = (P("dp", None, "tensor"), P("dp", None, "tensor"), P("tensor", None))
    return jax.shard_map(
        on_device,
        mesh=mesh,
        in_specs=placed,
        out_specs=(P("dp", None, "tensor"), P("tensor", None)),
        check_vma=False,
    )
```

```python
import jax
import jax.numpy as jnp
from jax import lax
from jax.experimental import pallas as pl
from jax.experimental.pallas import tpu as pltpu
from jax.sharding import PartitionSpec as P

F32, BF16 = jnp.float32, jnp.bfloat16
LANES = 128
CHIPS = 16
MAIN = 160
MIXED = 32
ORDERS = (
    [10, 11, 8, 13, 14, 0, 9, 7, 6, 15, 1, 3, 2, 12, 4, 5],
    [5, 6, 10, 11, 8, 4, 7, 0, 1, 15, 2, 3, 13, 14, 9, 12],
)
VMEM_LIMIT = 48 * 1024 * 1024
SENT_LIMIT = 52 * 1024 * 1024
KEPT_LIMIT = 52 * 1024 * 1024


def params():
    return pltpu.CompilerParams(vmem_limit_bytes=VMEM_LIMIT)


def combined_half(which, g_in, e_in, out_ref, g_ref, e_ref, sems):
    half, cols = g_ref.shape
    chunks = sems.shape[1]
    count = half // chunks
    copies = []
    for chunk in range(chunks):
        rows = pl.ds(pl.multiple_of(which * half + chunk * count, 16), count)
        here = slice(chunk * count, (chunk + 1) * count)
        pair = [
            pltpu.make_async_copy(g_in.at[rows, :], g_ref.at[here, :], sems.at[0, chunk]),
            pltpu.make_async_copy(e_in.at[rows, :], e_ref.at[here, :], sems.at[1, chunk]),
        ]
        for copy in pair:
            copy.start()
        copies.append(pair)
    for chunk in range(chunks):
        for copy in copies[chunk]:
            copy.wait()
        here = slice(chunk * count, (chunk + 1) * count)
        total = (g_ref[here, :].astype(F32) + e_ref[here, :].astype(F32)).astype(BF16)
        for slab in range(cols // LANES):
            first = slab * half + chunk * count
            out_ref[first : first + count, :] = total[:, slab * LANES : (slab + 1) * LANES]


def sent_kernel(core_ref, g_in, e_in, out_ref, *scratch):
    combined_half(1 - core_ref[0], g_in, e_in, out_ref, *scratch)


def kept_kernel(core_ref, g_in, e_in, q_ref, out_ref, p_ref, *scratch):
    combined_half(core_ref[0], g_in, e_in, out_ref, *scratch)
    p_ref[...] = slab_product(out_ref, q_ref, p_ref.shape[0])


def slab_product(slabs_ref, q_ref, half):
    p = jnp.zeros((half, LANES), F32)
    for pair in range(q_ref.shape[0] // (2 * LANES)):
        two = [slabs_ref[(2 * pair + k) * half : (2 * pair + k + 1) * half, :] for k in range(2)]
        q = q_ref[2 * pair * LANES : 2 * (pair + 1) * LANES, :]
        p += jnp.dot(jnp.concatenate(two, axis=1), q, preferred_element_type=F32)
    return p


def half_call(kernel, limit, core, gradient, error, *more):
    rows, cols = gradient.shape
    half = rows // 2
    chunks = 2
    out = jax.ShapeDtypeStruct((cols // LANES * half, LANES), BF16)
    vmem = pl.BlockSpec(memory_space=pltpu.VMEM)
    anywhere = pl.BlockSpec(memory_space=pl.ANY)
    return pl.pallas_call(
        kernel,
        out_shape=(out, jax.ShapeDtypeStruct((half, LANES), F32)) if more else out,
        in_specs=[pl.BlockSpec(memory_space=pltpu.SMEM), anywhere, anywhere] + [vmem] * len(more),
        out_specs=(vmem, vmem) if more else vmem,
        scratch_shapes=[
            pltpu.VMEM((half, cols), BF16),
            pltpu.VMEM((half, cols), BF16),
            pltpu.SemaphoreType.DMA((2, chunks)),
        ],
        compiler_params=pltpu.CompilerParams(vmem_limit_bytes=limit),
        name="kept" if more else "sent",
    )(core, gradient, error, *more)


def upper_rows():
    return lax.broadcasted_iota(jnp.int32, (8, LANES), 0) < 4


def swap(x):
    return jnp.concatenate([x[4:, :], x[:4, :]], axis=0)


def high_low(x):
    high = x.astype(BF16).astype(F32)
    return high, x - high


def joined(eight, four):
    high, low = high_low(eight)
    high4, low4 = high_low(four)
    return jnp.concatenate([high, low, jnp.where(upper_rows(), high4, low4)], axis=0)


def parted(x):
    return x[:8, :] + x[8:16, :], x[16:, :] + swap(x[16:, :])


def pack_kernel(own_ref, got_ref, p_ref, q_ref, out_ref):
    half = p_ref.shape[0]
    p = p_ref[...] + slab_product(got_ref, q_ref, half)
    for piece in range(CHIPS):
        rows = slice(piece * MAIN, (piece + 1) * MAIN)
        out_ref[piece, :MAIN, :] = (own_ref[rows, :].astype(F32) + got_ref[rows, :].astype(F32)).astype(BF16)
    last = slice(CHIPS * MAIN, CHIPS * (MAIN + 8))
    extra = own_ref[last, :].astype(F32) + got_ref[last, :].astype(F32)
    for piece in range(CHIPS):
        both = p[8 * (CHIPS + piece // 2) : 8 * (CHIPS + piece // 2 + 1), :]
        four = jnp.where(upper_rows() == (piece % 2 == 0), both, swap(both))
        mixed = [extra[8 * piece : 8 * piece + 8, :], joined(p[8 * piece : 8 * piece + 8, :], four)]
        out_ref[piece, MAIN:, :] = jnp.concatenate(mixed, axis=0).astype(BF16)


def pack(own, got, p_own, q_prev):
    return pl.pallas_call(
        pack_kernel,
        out_shape=jax.ShapeDtypeStruct((CHIPS, MAIN + MIXED, LANES), BF16),
        compiler_params=params(),
        name="pack",
    )(own, got, p_own, q_prev)


def sums_kernel(in_ref, left_ref, total_ref):
    total = in_ref[0].astype(F32)
    for chip in range(1, CHIPS):
        total += in_ref[chip].astype(F32)
    left = joined(*parted(total[MAIN + 8 :, :])).astype(BF16)
    for copy in range(left_ref.shape[0]):
        left_ref[copy] = left
    total_ref[...] = total[: MAIN + 8, :]


def sums(pieces, copies):
    return pl.pallas_call(
        sums_kernel,
        out_shape=(
            jax.ShapeDtypeStruct((copies, MIXED - 8, LANES), BF16),
            jax.ShapeDtypeStruct((MAIN + 8, LANES), F32),
        ),
        compiler_params=params(),
        name="sums",
    )(pieces)


def repack_kernel(left_ref, total_ref, out_ref):
    left = left_ref[0].astype(F32)
    for at in range(1, left_ref.shape[0]):
        left += left_ref[at].astype(F32)
    piece = jnp.concatenate([total_ref[...], joined(*parted(left))], axis=0).astype(BF16)
    for chip in range(CHIPS):
        out_ref[chip] = piece


def repack(left, total):
    return pl.pallas_call(
        repack_kernel,
        out_shape=jax.ShapeDtypeStruct((CHIPS, MAIN + MIXED, LANES), BF16),
        compiler_params=params(),
        name="repack",
    )(left, total)


def spread(x, row=None, lane=None):
    if row is not None:
        x = x[row : row + 1, :]
    if lane is not None:
        x = x[:, lane : lane + 1]
    return jnp.broadcast_to(x, (8, LANES))


def added(terms):
    while len(terms) > 1:
        terms = [terms[i] + terms[i + 1] for i in range(0, len(terms), 2)]
    return terms[0]


def inverse_factor(gram):
    width = 8
    groups = LANES // width
    w = [gram[width * g : width * (g + 1), :] for g in range(groups)]
    row_of = lax.broadcasted_iota(jnp.int32, (width, LANES), 0)
    lane_of = lax.broadcasted_iota(jnp.int32, (width, LANES), 1)
    pivots = [spread(w[0], lane=i) for i in range(width)]
    for g in range(groups):
        first = width * g
        more = g + 1 < groups
        column = {h: [spread(w[h], lane=first + i) for i in range(width)] for h in range(g + 1, groups)}
        ahead = [spread(w[g + 1], lane=first + width + n) for n in range(width)] if more else []
        inside = (lane_of >= first) & (lane_of < first + width)
        start = jnp.where(inside, jnp.where(lane_of - first == row_of, 1.0, 0.0), w[g])
        y = [spread(start, row=m) for m in range(width)]
        d = [[spread(pivots[i], row=m) for i in range(m + 1)] for m in range(width)]
        low = [[None] * width for _ in range(width)]
        root = [None] * width
        lead = list(column[g + 1]) if more else None
        for i in range(width):
            if i % 2 == 0:
                first_root = lax.rsqrt(d[i][i])
                det = d[i][i] * d[i + 1][i + 1] - d[i + 1][i] * d[i + 1][i]
                root[i] = first_root
                root[i + 1] = d[i][i] * first_root * lax.rsqrt(det)
            for m in range(i + 1, width):
                low[m][i] = d[m][i] * root[i]
            for m in range(i + 1, width):
                for n in range(i + 1, m + 1):
                    if i % 2 == 1 or m > i + 1:
                        d[m][n] = d[m][n] - low[m][i] * low[n][i]
            y[i] = y[i] * root[i]
            for m in range(i + 1, width):
                y[m] = y[m] - low[m][i] * y[i]
            if more:
                lead[i] = lead[i] * root[i]
                for m in range(i + 1, width):
                    lead[m] = lead[m] - low[m][i] * lead[i]
        z = [None] * width
        for m in reversed(range(width)):
            value = y[m]
            for k in range(m + 1, width):
                value = value - low[k][m] * z[k]
            z[m] = value * root[m]
        for h in range(g + 1, groups):
            left, right = (lead, y) if h == g + 1 else (column[h], z)
            w[h] = jnp.where(inside, 0.0, w[h]) - added([left[i] * right[i] for i in range(width)])
        pivots = [
            ahead[n] - added([lead[i] * spread(lead[i], row=n) for i in range(width)]) for n in range(len(ahead))
        ]
        rows = y[0]
        for m in range(1, width):
            rows = jnp.where(row_of == m, y[m], rows)
        w[g] = jnp.where(lane_of <= row_of + first, rows, 0.0)
    return jnp.concatenate(w, axis=0)


def left_half(ref):
    parts = [parted(ref[piece, MAIN:, :].astype(F32)[8:, :]) for piece in range(CHIPS)]
    lower = [jnp.where(upper_rows(), parts[2 * k][1], parts[2 * k + 1][1]) for k in range(CHIPS // 2)]
    return jnp.concatenate([eight for eight, _ in parts] + lower, axis=0)


def flipped_basis(p):
    def product(x, y):
        return jnp.dot(x, y, precision=lax.Precision.HIGHEST, preferred_element_type=F32)

    p = p * lax.rsqrt(jnp.sum(p * p, axis=0, keepdims=True))
    flipped = p.T
    return product(inverse_factor(product(flipped, p)), flipped)


def finish_kernel(
    replicas,
    core_ref,
    own_ref,
    other_ref,
    own_sum_ref,
    other_sum_ref,
    error_out,
    q_out,
    error_ref,
    q_ref,
    basis_ref,
    sems,
):
    core = core_ref[0]
    half = basis_ref.shape[1]

    def slab_of(ref, slab):
        at, end, parts = slab * half, (slab + 1) * half, []
        while at < min(end, CHIPS * MAIN):
            piece = at // MAIN
            stop = min(end, (piece + 1) * MAIN)
            parts.append(ref[piece, at - piece * MAIN : stop - piece * MAIN, :])
            at = stop
        if at < end:
            extra = [ref[piece, MAIN : MAIN + 16, :].astype(F32)[:8, :] for piece in range(CHIPS)]
            parts.append(jnp.concatenate(extra, axis=0).astype(BF16))
        return jnp.concatenate(parts, axis=0)

    def pair_of(read, pair):
        return jnp.concatenate([read(2 * pair), read(2 * pair + 1)], axis=1)

    is_first = core == 0

    def in_order(own, other):
        return jnp.concatenate([jnp.where(is_first, own, other), jnp.where(is_first, other, own)], axis=0)

    flipped = flipped_basis(in_order(left_half(own_sum_ref), left_half(other_sum_ref)))
    rows_of_basis = flipped.T.astype(BF16)
    flipped = flipped.astype(BF16)
    basis_ref[0] = rows_of_basis[:half, :]
    basis_ref[1] = rows_of_basis[half:, :]
    basis = (basis_ref[core], basis_ref[1 - core])
    copies = []
    pairs = q_ref.shape[0] // (2 * LANES)

    def right_of(pair):
        sums = in_order(*(pair_of(lambda slab: slab_of(ref, slab), pair) for ref in (own_sum_ref, other_sum_ref)))
        return jnp.dot(flipped, sums, preferred_element_type=F32) * (1.0 / replicas)

    def send(source, target, sem):
        copies.append(pltpu.make_async_copy(source, target, sem))
        copies[-1].start()

    ready = [right_of(pair) for pair in range(2)]
    for pair in range(pairs):
        columns = slice(2 * pair * LANES, 2 * (pair + 1) * LANES)
        scaled = ready.pop(0)
        right = scaled.astype(BF16)
        if pair + 2 < pairs:
            ready.append(right_of(pair + 2))
        products = [jnp.dot(b, right, preferred_element_type=F32) for b in basis]
        for at, (which, ref) in enumerate(((core, own_ref), (1 - core, other_ref))):
            mine = pair_of(lambda slab: ref[slab * half : (slab + 1) * half, :], pair).astype(F32)
            rows = pl.ds(pl.multiple_of(which * half, half), half)
            error_ref[rows, columns] = (mine - products[at]).astype(BF16)
            send(error_ref.at[rows, columns], error_out.at[rows, columns], sems.at[at, pair])
        q_ref[columns, :] = scaled.T.astype(BF16)
        send(q_ref.at[columns, :], q_out.at[columns, :], sems.at[2, pair])
    for copy in copies:
        copy.wait()


def finish(core, own, other, own_sum, other_sum, rows, cols, replicas):
    vmem = pl.BlockSpec(memory_space=pltpu.VMEM)
    return pl.pallas_call(
        lambda *refs: finish_kernel(replicas, *refs),
        out_shape=(jax.ShapeDtypeStruct((rows, cols), BF16), jax.ShapeDtypeStruct((cols, LANES), BF16)),
        in_specs=[pl.BlockSpec(memory_space=pltpu.SMEM)] + [vmem] * 4,
        out_specs=(pl.BlockSpec(memory_space=pl.ANY),) * 2,
        scratch_shapes=[
            pltpu.VMEM((rows, cols), BF16),
            pltpu.VMEM((cols, LANES), BF16),
            pltpu.VMEM((2, rows // 2, LANES), BF16),
            pltpu.SemaphoreType.DMA((3, cols // (2 * LANES))),
        ],
        compiler_params=params(),
        name="finish",
    )(core, own, other, own_sum, other_sum)


def on_device(gradient, error, q_prev):
    rows, cols = gradient.shape[1:]
    replicas = lax.axis_size("dp")
    half = rows // 2
    core = (lax.axis_index("dp") % 2).astype(jnp.int32).reshape(1)
    twin = [(i, i ^ 1) for i in range(replicas)]
    same_core = [[2 * chip + c for chip in ORDERS[c]] for c in range(2)]

    def across_chips(pieces):
        return lax.all_to_all(pieces, "dp", 0, 0, axis_index_groups=same_core)

    other = half_call(sent_kernel, SENT_LIMIT, core, gradient[0], error[0])
    got = lax.ppermute(other, "dp", twin)
    own, p_own = half_call(kept_kernel, KEPT_LIMIT, core, gradient[0], error[0], q_prev)
    pieces = across_chips(pack(own, got, p_own, q_prev))
    left, total = sums(pieces, lax.axis_size("tensor"))
    left = lax.all_to_all(left, "tensor", 0, 0)
    gathered = across_chips(repack(left, total))
    gathered_other = lax.ppermute(gathered, "dp", twin)
    new_error, q_next = finish(core, own, other, gathered, gathered_other, rows, cols, replicas)
    return (new_error[None], q_next)


def solution(mesh):
    placed = (P("dp", None, "tensor"), P("dp", None, "tensor"), P("tensor", None))
    return jax.shard_map(
        on_device,
        mesh=mesh,
        in_specs=placed,
        out_specs=(P("dp", None, "tensor"), P("tensor", None)),
        check_vma=False,
    )
```
